256 devices in a mesh: seq: 32 (over y, z), kvh: 8 (over x, core).
Axes of the slice: x: 4, y: 4, z: 8, core: 2. Of those that a mesh axis runs over, the one named last changes fastest.
Arguments:
- queries: bfloat16 [16384, 64, 128], P('seq', 'kvh'), may hold values from -24 to 24, as said below
- keys: bfloat16 [16384, 8, 128], P('seq', 'kvh'), may hold values from -24 to 24, as said below
- values: bfloat16 [16384, 8, 128], P('seq', 'kvh'), may hold values from -6 to 6
- teacher: bfloat16 [16384, 64, 128], P('seq', 'kvh'), may hold values from -6 to 6
- q_map: bfloat16 [64, 128, 64], P('kvh'), as said below
- k_map: bfloat16 [64, 128, 64], P('kvh'), as said below
Outputs:
- attn_out: bfloat16 [16384, 64, 128], P('seq', 'kvh')
- grad_q_map: float32 [64, 128, 64], P('kvh')
- grad_k_map: float32 [64, 128, 64], P('kvh')
- loss: float32 [], replicated
The draws below stay inside these ranges and needn't reach their ends.
Inputs may be any that keep to these rules, and one draw needn't show every extreme that they name: `queries`: Real-valued entries. `keys`: Real-valued entries. `q_map`: Real-valued entries. `k_map`: Real-valued entries.
All inputs are finite; a program needn't handle non-finite values.
Results may differ from the reference program's by a relative error of at most 0.001.
Values may be sent and summed in bfloat16 or wider, within the bound.
A program may use at most 128 MiB of HBM per device.

```python
import jax
import jax.numpy as jnp
from jax import lax

HD = 128
FEAT = 128
WIN = 64
TOK_DEV = 512
TOKENS = 16384
KVH = 8
QH = 64


def maps_common(key, salt):
    base = jax.random.normal(jax.random.fold_in(key, salt), (QH, HD, FEAT // 2), jnp.float32)
    return jnp.clip(base, -4.0, 4.0) * HD ** (-0.5)


def draw_q_map(key, part):
    return maps_common(key, 101).astype(jnp.bfloat16)


def draw_k_map(key, part):
    return maps_common(key, 202).astype(jnp.bfloat16)


def draw_queries(key, part):
    base = jnp.clip(jax.random.normal(jax.random.fold_in(key, 404), (TOKENS, QH, HD), jnp.float32), -6.0, 6.0)
    return base.astype(jnp.bfloat16)


def draw_keys(key, part):
    base = jnp.clip(jax.random.normal(jax.random.fold_in(key, 505), (TOKENS, KVH, HD), jnp.float32), -6.0, 6.0)
    return base.astype(jnp.bfloat16)


def level_of(stream_key, dims, split, least, top_value):
    gain, own = 1.0, jax.random.fold_in(stream_key, 6)
    for dim, shards_of in split:
        steps = jnp.exp(jax.random.uniform(jax.random.fold_in(own, dim), (shards_of,), jnp.float32, least / len(split), top_value / len(split)))
        gain = gain * jnp.repeat(steps, dims[dim] // shards_of).reshape([-1 if axis == dim else 1 for axis in range(len(dims))])
    return gain


def scatter_about(key, extent, scale, bound, split=(), kind=jnp.bfloat16):
    loudness = level_of(key, extent, split, -0.22, 0.18) if split else 1.0
    drawn = jax.random.normal(key, extent, jnp.float32) * scale * loudness
    return jnp.minimum(jnp.maximum(drawn, -bound), bound).astype(kind)


def setup_inputs(seed: int = 0) -> dict:
    key_of = jax.random.split(jax.random.key(seed), 7)
    return {
        "queries": draw_queries(jax.random.fold_in(key_of[6], 71), 0),
        "keys": draw_keys(jax.random.fold_in(key_of[6], 71), 0),
        "values": scatter_about(key_of[2], (TOKENS, KVH, HD), 1.0, 6.0, ((0, 32), (1, 8))),
        "teacher": scatter_about(key_of[3], (TOKENS, QH, HD), 1.0, 6.0, ((0, 32), (1, 8))),
        "q_map": draw_q_map(jax.random.fold_in(key_of[6], 71), 0),
        "k_map": draw_k_map(jax.random.fold_in(key_of[6], 71), 0),
    }


def features(rows, weights):
    scores = jnp.dot(rows.astype(jnp.float32), weights, precision=lax.Precision.HIGHEST, preferred_element_type=jnp.float32)
    return jnp.concatenate([jax.nn.softmax(scores, axis=-1), jax.nn.softmax(-scores, axis=-1)], axis=-1)

def hdot(left, right):
    return jnp.dot(left, right, precision=lax.Precision.HIGHEST, preferred_element_type=jnp.float32)

def reference(queries, keys, values, teacher, q_map, k_map):
    total, heads, width = queries.shape
    group = heads // keys.shape[1]
    block = min(TOK_DEV, 128)
    count = total // block
    scale = width ** (-0.5)
    pad_keys = jnp.concatenate([jnp.zeros((WIN,) + keys.shape[1:], keys.dtype), keys], axis=0)
    pad_vals = jnp.concatenate([jnp.zeros((WIN,) + values.shape[1:], jnp.float32), values.astype(jnp.float32)], axis=0)

    def one_head(head, q_weights, k_weights):
        kv_index = (head // group).astype(jnp.int32)
        q_head = lax.dynamic_index_in_dim(queries, head, 1, keepdims=False)
        k_head = lax.dynamic_index_in_dim(pad_keys, kv_index, 1, keepdims=False)
        v_head = lax.dynamic_index_in_dim(pad_vals, kv_index, 1, keepdims=False)
        w_query = lax.dynamic_index_in_dim(q_weights, head, 0, keepdims=False)
        w_key = lax.dynamic_index_in_dim(k_weights, head, 0, keepdims=False)

        def step(carry, blk):
            state, norm = carry
            start = (blk * block).astype(jnp.int32)
            q_blk = lax.dynamic_slice_in_dim(q_head, start, block, 0)
            k_blk = lax.dynamic_slice_in_dim(k_head, start, block + WIN, 0)
            v_blk = lax.dynamic_slice_in_dim(v_head, start, block + WIN, 0)
            q_pos = start + jnp.arange(block, dtype=jnp.int32)
            k_pos = start - WIN + jnp.arange(block + WIN, dtype=jnp.int32)
            near_mask = (k_pos[None, :] > q_pos[:, None] - WIN) & (k_pos[None, :] <= q_pos[:, None]) & (k_pos[None, :] >= 0)
            far_mask = ((k_pos[None, :] <= q_pos[:, None] - WIN) & (k_pos[None, :] >= 0)).astype(jnp.float32)
            q_feat = features(q_blk, w_query)
            k_feat = features(k_blk, w_key)
            scores = jnp.dot(q_blk, k_blk.T, preferred_element_type=jnp.float32) * scale
            scores = jnp.where(near_mask, scores, -1e+30)
            top = lax.optimization_barrier(jnp.max(scores, axis=-1, keepdims=True))
            weights = jnp.where(near_mask, jnp.exp(scores - top), 0.0)
            far = hdot(q_feat, k_feat.T) * far_mask
            numer = hdot(weights + far, v_blk) + hdot(q_feat, state)
            denom = lax.optimization_barrier(jnp.sum(weights + far, axis=-1)) + hdot(q_feat, norm)
            out = numer / denom[:, None]
            keep = (k_pos[:block] >= 0).astype(jnp.float32)
            kept = k_feat[:block] * keep[:, None]
            state = state + hdot(kept.T, v_blk[:block])
            norm = norm + lax.optimization_barrier(jnp.sum(kept, axis=0))
            return ((state, norm), out)
        init = (jnp.zeros((FEAT, width), jnp.float32), jnp.zeros((FEAT,), jnp.float32))
        _, outs = lax.scan(jax.checkpoint(step), init, jnp.arange(count, dtype=jnp.int32))
        return outs.reshape(total, width)

    def forward(q_weights, k_weights):

        def per_head(head):
            return one_head(head, q_weights, k_weights)
        outs = lax.map(per_head, jnp.arange(heads, dtype=jnp.int32))
        error = outs - jnp.swapaxes(teacher, 0, 1).astype(jnp.float32)
        return (jnp.sum(error * error) / total, outs)
    loss, pullback, outs = jax.vjp(forward, q_map.astype(jnp.float32), k_map.astype(jnp.float32), has_aux=True)
    grad_q, grad_k = pullback(jnp.ones_like(loss))
    return (jnp.swapaxes(outs, 0, 1).astype(jnp.bfloat16), grad_q, grad_k, loss)
```

```python
import functools

import jax
import jax.numpy as jnp
from jax import lax
from jax.experimental import pallas as pl
from jax.experimental.pallas import tpu as pltpu
from jax.sharding import PartitionSpec as P

WIN = 64
BLK = 128
F32, BF16 = jnp.float32, jnp.bfloat16
MESH = pl.DeviceIdType.MESH


def split(x):
    hi = x.astype(BF16)
    return hi, (x - hi.astype(F32)).astype(BF16)


def nn(a, b):
    return lax.dot_general(a, b, (((1,), (0,)), ((), ())), preferred_element_type=F32)


def nt(a, b):
    return lax.dot_general(a, b, (((1,), (1,)), ((), ())), preferred_element_type=F32)


def lanes(*parts):
    return jnp.concatenate(parts, axis=1)


def rows(*parts):
    return jnp.concatenate(parts, axis=0)


def peers(n, fn):
    def go(i, carry):
        fn(i)
        return carry

    lax.fori_loop(1, n, go, 0)


def remote(src, dst, send, recv, dev, axis="seq"):
    return pltpu.make_async_remote_copy(
        src_ref=src, dst_ref=dst, send_sem=send, recv_sem=recv, device_id={axis: dev}, device_id_type=MESH
    )


class Scan:
    def __init__(self, n, me, own, own_norm, got, part, out, got_norm, part_norm, out_norm, sems, norm_sems, reverse):
        self.__dict__.update(locals())
        self.chunk = own.shape[0] // n
        self.keeper = n // 2

    def piece(self, dev):
        return pl.ds(pl.multiple_of(dev * self.chunk, 8), self.chunk)

    def first(self, dev, src):
        return remote(self.own.at[self.piece(dev)], self.got.at[src], self.sems.at[0, dev], self.sems.at[1, src], dev)

    def second(self, dev, src):
        return remote(self.part.at[dev], self.out.at[self.piece(src)], self.sems.at[2, dev], self.sems.at[3, src], dev)

    def norm_first(self, src):
        return remote(self.own_norm, self.got_norm.at[src], self.norm_sems.at[0, 0], self.norm_sems.at[1, src], self.keeper)

    def norm_second(self, dev):
        return remote(self.part_norm.at[dev], self.out_norm, self.norm_sems.at[2, dev], self.norm_sems.at[0, 1], dev)

    def start(self):
        n, me = self.n, self.me

        @pl.when(me != self.keeper)
        def _():
            self.norm_first(me).start()

        peers(n, lambda i: self.first(lax.rem(me + i, n), me).start())

    def sums(self, got, part, zero):
        n = self.n

        def go(i, total):
            at = n - 1 - i if self.reverse else i
            part[at] = total
            return total + got[at]

        lax.fori_loop(0, n, go, zero)

    def turn(self):
        n, me, keeper = self.n, self.me, self.keeper
        self.got[me] = self.own[self.piece(me)]
        peers(n, lambda i: self.first(me, lax.rem(me + i, n)).wait_recv())
        self.sums(self.got, self.part, jnp.zeros((self.chunk, 128), F32))
        peers(n, lambda i: self.second(lax.rem(me + i, n), me).start())
        self.out[self.piece(me)] = self.part[me]

        @pl.when(me == keeper)
        def _():
            self.got_norm[keeper] = self.own_norm[...]
            peers(n, lambda i: self.norm_first(lax.rem(keeper + i, n)).wait_recv())
            self.sums(self.got_norm, self.part_norm, jnp.zeros((8, 128), F32))
            peers(n, lambda i: self.norm_second(lax.rem(keeper + i, n)).start())
            self.out_norm[...] = self.part_norm[keeper]

    def finish(self):
        n, me = self.n, self.me
        peers(n, lambda i: self.second(me, lax.rem(me + i, n)).wait_recv())

        @pl.when(me != self.keeper)
        def _():
            self.norm_second(me).wait_recv()

    def drain(self):
        n, me, keeper = self.n, self.me, self.keeper

        def one(i):
            dev = lax.rem(me + i, n)
            self.first(dev, me).wait_send()
            self.second(dev, me).wait_send()

        peers(n, one)

        @pl.when(me != keeper)
        def _():
            self.norm_first(me).wait_send()

        @pl.when(me == keeper)
        def _():
            peers(n, lambda i: self.norm_second(lax.rem(keeper + i, n)).wait_send())


class Total:
    def __init__(self, n, me, own, got, part, out, sems):
        self.__dict__.update(locals())
        self.chunk = own.shape[0] // n

    def piece(self, dev):
        return pl.ds(pl.multiple_of(dev * self.chunk, 8), self.chunk)

    def first(self, dev, src):
        return remote(self.own.at[self.piece(dev)], self.got.at[src], self.sems.at[0, dev], self.sems.at[1, src], dev)

    def second(self, dev, src):
        return remote(self.part, self.out.at[self.piece(src)], self.sems.at[2, dev], self.sems.at[3, src], dev)

    def start(self):
        peers(self.n, lambda i: self.first(lax.rem(self.me + i, self.n), self.me).start())

    def turn(self):
        n, me = self.n, self.me
        self.got[me] = self.own[self.piece(me)]
        peers(n, lambda i: self.first(me, lax.rem(me + i, n)).wait_recv())
        self.part[...] = lax.fori_loop(0, n, lambda i, t: t + self.got[i], jnp.zeros((self.chunk, 128), F32))
        peers(n, lambda i: self.second(lax.rem(me + i, n), me).start())
        self.out[self.piece(me)] = self.part[...]

    def finish(self):
        n, me = self.n, self.me
        peers(n, lambda i: self.second(me, lax.rem(me + i, n)).wait_recv())

    def drain(self):
        n, me = self.n, self.me

        def one(i):
            dev = lax.rem(me + i, n)
            self.first(dev, me).wait_send()
            self.second(dev, me).wait_send()

        peers(n, one)


def kernel(n, m, heads, tok, scale, inv_total, q_ref, k_ref, v_ref, t_ref, wq_ref, wk_ref,
           y_ref, gq_ref, gk_ref, loss_ref,
           tmp, kext, vext, vaug, vaugt, kt, qh, pqh, pql, pkh, pkl,
           s_own, s_norm, s_got, s_part, s_in, sn_got, sn_part, sn_in,
           loc, loc_norm, numer, gn_s, gd_s, dblk, dblk_norm,
           d_own, d_norm, d_got, d_part, d_in, dn_got, dn_part, dn_in,
           gkf, aq, aq_got, aq_part, aq_out, ak, ak_got, ak_part, ak_out,
           loss_own, loss_kv, loss_row, loss_seq,
           f_sems, fn_sems, b_sems, bn_sems, q_sems, k_sems, e_sems, lk_sems, ls_sems):
    me = lax.axis_index("seq")
    col = lax.axis_index("kvh")
    nblk = tok // BLK
    half = heads // 2

    barrier = pltpu.get_barrier_semaphore()
    peers(n, lambda i: pl.semaphore_signal(barrier, inc=1, device_id={"seq": lax.rem(me + i, n)}, device_id_type=MESH))
    peers(m, lambda i: pl.semaphore_signal(barrier, inc=1, device_id={"kvh": lax.rem(col + i, m)}, device_id_type=MESH))

    lane = lax.broadcasted_iota(jnp.int32, (1, 128), 1)
    upper = lane < 64
    ri = lax.broadcasted_iota(jnp.int32, (256, 128), 0)
    ci = lax.broadcasted_iota(jnp.int32, (256, 128), 1)
    ones2 = jnp.where((lax.rem(ri, 128) < 64) == (ci < 64), 1.0, 0.0).astype(BF16)

    def half_sums(x):
        hi, lo = split(x)
        return nn(lanes(hi, lo), ones2)

    def maps(x, w):
        w = w.astype(F32)
        a = nn(x, lanes(w, -w).astype(BF16))
        low = jnp.full_like(a, -jnp.inf)
        top = jnp.where(
            upper,
            jnp.max(jnp.where(upper, a, low), axis=-1, keepdims=True),
            jnp.max(jnp.where(upper, low, a), axis=-1, keepdims=True),
        )
        e = jnp.exp(a - top)
        return e / half_sums(e)

    def back(phi, g):
        return phi * (g - half_sums(phi * g))

    kext[WIN : WIN + tok] = k_ref[...]
    vext[WIN : WIN + tok] = v_ref[...]
    vt = v_ref[...].astype(F32).T.astype(BF16)
    vt2 = lanes(vt, vt)

    def own_keys(h, carry):
        phi = maps(k_ref[...], wk_ref[h])
        hi, lo = split(phi)
        pkh[h, WIN : WIN + tok] = hi
        pkl[h, WIN : WIN + tok] = lo
        s_own[pl.ds(pl.multiple_of(h * 128, 128), 128)] = nn(vt2, rows(hi, lo))
        s_norm[pl.ds(h, 1)] = jnp.sum(phi, axis=0, keepdims=True)
        return carry

    lax.fori_loop(0, heads, own_keys, 0)
    pl.semaphore_wait(barrier, n - 1 + m - 1)

    def edge_copy(i, dev):
        src, dst = (k_ref, kext) if i == 0 else (v_ref, vext)
        return remote(src.at[pl.ds(tok - WIN, WIN)], dst.at[pl.ds(0, WIN)], e_sems.at[0, i], e_sems.at[1, i], dev)

    @pl.when(me < n - 1)
    def _():
        edge_copy(0, me + 1).start()
        edge_copy(1, me + 1).start()

    fwd = Scan(n, me, s_own, s_norm, s_got, s_part, s_in, sn_got, sn_part, sn_in, f_sems, fn_sems, False)
    bwd = Scan(n, me, d_own, d_norm, d_got, d_part, d_in, dn_got, dn_part, dn_in, b_sems, bn_sems, True)
    fwd.start()

    tmp[...] = q_ref[...].astype(F32)

    def query_maps(h, carry):
        x = tmp[pl.ds(h, tok, stride=heads), :].astype(BF16)
        qh[h] = x
        hi, lo = split(maps(x, wq_ref[h]))
        pqh[h] = hi
        pql[h] = lo
        return carry

    lax.fori_loop(0, heads, query_maps, 0)

    @pl.when(me == 0)
    def _():
        kext[0:WIN] = jnp.zeros((WIN, 128), BF16)
        vext[0:WIN] = jnp.zeros((WIN, 128), BF16)

    @pl.when(me > 0)
    def _():
        edge_copy(0, me - 1).wait_recv()
        edge_copy(1, me - 1).wait_recv()

    pad = jnp.zeros((WIN, 128), BF16)
    kext[WIN + tok :] = pad
    vext[WIN + tok :] = pad
    valid = jnp.where(me > 0, 1.0, 0.0).astype(F32)
    vaug[:, 0:128] = vext[...]
    vaug[:, 128:256] = jnp.ones((tok + 2 * WIN, 128), BF16)
    vaugt[0:128] = vext[0:tok].astype(F32).T.astype(BF16)
    vaugt[128:256] = jnp.ones((128, tok), BF16)
    kt[...] = kext[0:tok].astype(F32).T.astype(BF16)

    def edge_maps(h, carry):
        phi = maps(kext[0:WIN], wk_ref[h]) * valid
        hi, lo = split(phi)
        pkh[h, 0:WIN] = hi
        pkl[h, 0:WIN] = lo
        return carry

    lax.fori_loop(0, heads, edge_maps, 0)
    fwd.turn()

    r2 = lax.broadcasted_iota(jnp.int32, (BLK, 2 * BLK), 0)
    c2 = lax.broadcasted_iota(jnp.int32, (BLK, 2 * BLK), 1)
    near_band = (c2 > r2) & (c2 <= r2 + WIN)
    first_key = jnp.where(me > 0, 0, WIN)
    r1 = lax.broadcasted_iota(jnp.int32, (BLK, BLK), 0)
    c1 = lax.broadcasted_iota(jnp.int32, (BLK, BLK), 1)
    causal = c1 <= r1

    def local_forward(h, carry):
        ph0 = pkh[h, 0:WIN]
        pl0 = pkl[h, 0:WIN]
        zero = jnp.zeros((WIN, 128), BF16)
        vb = vaugt[:, 0:BLK]
        state = -nn(lanes(vb, vb), rows(ph0, zero, pl0, zero))
        for b in range(nblk):
            at = b * BLK
            loc[h, b] = state[0:128]
            loc_norm[h, b] = state[128:136]
            kh = pkh[h, at : at + BLK]
            kl = pkl[h, at : at + BLK]
            qhi = pqh[h, at : at + BLK]
            qlo = pql[h, at : at + BLK]
            q3 = lanes(qhi, qlo, qhi)
            far = jnp.where(causal, nt(q3, lanes(kh, kh, kl)), 0.0)
            s = nt(qh[h, at : at + BLK], kext[at : at + 2 * BLK]) * scale
            mask = near_band & (c2 >= first_key) if b == 0 else near_band
            s = jnp.where(mask, s, -1e30)
            top = jnp.max(s, axis=-1, keepdims=True)
            w = jnp.where(mask, jnp.exp(s - top), 0.0)
            w = lanes(w[:, 0:BLK] + far, w[:, BLK:])
            whi, wlo = split(w)
            va = vaug[at : at + 2 * BLK]
            shi, slo = split(state)
            numer[h, at : at + BLK] = nn(lanes(whi, wlo), rows(va, va)) + nt(q3, lanes(shi, shi, slo))
            if b + 1 < nblk:
                vb = vaugt[:, at : at + BLK]
                state = state + nn(lanes(vb, vb), rows(kh, kl))
        return carry

    lax.fori_loop(0, heads, local_forward, 0)
    fwd.finish()

    tmp[...] = t_ref[...].astype(F32)

    def outputs(h, squares):
        prior = s_in[pl.ds(pl.multiple_of(h * 128, 128), 128)]
        prior_norm = jnp.broadcast_to(sn_in[pl.ds(h, 1)], (128, 128))
        shi, slo = split(rows(prior, prior_norm))
        s3 = lanes(shi, shi, slo)
        d_sum = jnp.zeros((128, 128), F32)
        dn_sum = jnp.zeros((1, 128), F32)
        for b in range(nblk):
            at = b * BLK
            qhi = pqh[h, at : at + BLK]
            qlo = pql[h, at : at + BLK]
            both = numer[h, at : at + BLK] + nt(lanes(qhi, qlo, qhi), s3)
            den = both[:, 128:256]
            y = both[:, 0:128] / den
            where = pl.ds(h + at * heads, BLK, stride=heads)
            error = y - tmp[where, :]
            tmp[where, :] = y
            squares = squares + jnp.sum((error * error).reshape(BLK // 8, 8, 128), axis=0)
            gn = (2.0 * inv_total) * error / den
            gd = jnp.broadcast_to(-jnp.sum(gn * y, axis=-1, keepdims=True), (BLK, 128))
            gn_s[h, at : at + BLK] = gn
            gd_s[h, at : at + BLK] = gd
            ghi, glo = split(gn.T)
            d = nn(lanes(ghi, glo, ghi), rows(qhi, qhi, qlo))
            dn = jnp.sum(gd * (qhi.astype(F32) + qlo.astype(F32)), axis=0, keepdims=True)
            dblk[h, b] = d
            dblk_norm[h, b] = jnp.broadcast_to(dn, (8, 128))
            d_sum = d_sum + d
            dn_sum = dn_sum + dn
        d_own[pl.ds(pl.multiple_of(h * 128, 128), 128)] = d_sum
        d_norm[pl.ds(h, 1)] = dn_sum
        return squares

    loss_own[...] = lax.fori_loop(0, heads, outputs, jnp.zeros((8, 128), F32))
    bwd.start()

    def loss_cols(dev, src):
        return remote(loss_own, loss_kv.at[src], lk_sems.at[0, dev], lk_sems.at[1, src], dev, "kvh")

    def loss_rows(dev, src):
        return remote(loss_row, loss_seq.at[src], ls_sems.at[0, dev], ls_sems.at[1, src], dev)

    peers(m, lambda i: loss_cols(lax.rem(col + i, m), col).start())
    y_ref[...] = tmp[...].astype(BF16)

    def local_backward(h, carry):
        prior = s_in[pl.ds(pl.multiple_of(h * 128, 128), 128)]
        prior_norm = sn_in[pl.ds(h, 1)]
        later = jnp.zeros((128, 128), F32)
        later_norm = jnp.zeros((1, 128), F32)
        g = jnp.zeros((128, 128), F32)
        for b in reversed(range(nblk)):
            at = b * BLK
            gn = gn_s[h, at : at + BLK]
            gd = gd_s[h, at : at + BLK]
            vb = vext[at : at + BLK]
            kh = pkh[h, at : at + BLK]
            kl = pkl[h, at : at + BLK]
            qhi = pqh[h, at : at + BLK]
            qlo = pql[h, at : at + BLK]
            ghi, glo = split(gn)
            gf = jnp.where(causal, nt(lanes(ghi, glo), lanes(vb, vb)) + gd, 0.0)
            fhi, flo = split(gf)
            shi, slo = split(prior + loc[h, b])
            norm = prior_norm + loc_norm[h, b, 0:1]
            gqf = nn(lanes(fhi, flo, fhi, ghi, glo, ghi), rows(kh, kh, kl, shi, shi, slo)) + gd * norm
            rhi, rlo = split(back(qhi.astype(F32) + qlo.astype(F32), gqf))
            qt = qh[h, at : at + BLK].astype(F32).T.astype(BF16)
            g = g + nn(lanes(qt, qt), rows(rhi, rlo))
            thi, tlo = split(gf.T)
            lhi, llo = split(later)
            gkf[h, at : at + BLK] = (
                nn(lanes(thi, tlo, thi, vb, vb), rows(qhi, qhi, qlo, lhi, llo)) + later_norm
            )
            later = later + dblk[h, b]
            later_norm = later_norm + dblk_norm[h, b, 0:1]
        put(aq, h, g)
        return carry

    def put(ref, h, g):
        g = g - pltpu.roll(g, 64, 1)

        @pl.when(h < half)
        def _():
            ref[pl.ds(pl.multiple_of(h * 128, 128), 128)] = jnp.where(upper, g, 0.0)

        @pl.when(h >= half)
        def _():
            at = pl.ds(pl.multiple_of((h - half) * 128, 128), 128)
            ref[at] = jnp.where(upper, ref[at], -g)

    split_at = heads // 2
    lax.fori_loop(0, split_at, local_backward, 0)
    bwd.turn()
    lax.fori_loop(split_at, heads, local_backward, 0)
    q_total = Total(n, me, aq, aq_got, aq_part, aq_out, q_sems)
    k_total = Total(n, me, ak, ak_got, ak_part, ak_out, k_sems)
    q_total.start()
    loss_kv[col] = loss_own[...]
    peers(m, lambda i: loss_cols(col, lax.rem(col + i, m)).wait_recv())
    loss_row[...] = lax.fori_loop(0, m, lambda i, t: t + loss_kv[i], jnp.zeros((8, 128), F32))
    peers(n, lambda i: loss_rows(lax.rem(me + i, n), me).start())
    bwd.finish()

    def key_grads(h, carry):
        shi, slo = split(d_in[pl.ds(pl.multiple_of(h * 128, 128), 128)])
        suffix_norm = dn_in[pl.ds(h, 1)]
        v = vext[0:tok]
        g = gkf[h] + nn(lanes(v, v), rows(shi, slo)) + suffix_norm
        hi, lo = split(back(pkh[h, 0:tok].astype(F32) + pkl[h, 0:tok].astype(F32), g))
        t = kt[...]
        put(ak, h, nn(lanes(t, t), rows(hi, lo)))
        return carry

    lax.fori_loop(0, heads, key_grads, 0)
    k_total.start()
    q_total.turn()
    k_total.turn()

    loss_seq[me] = loss_row[...]
    peers(n, lambda i: loss_rows(me, lax.rem(me + i, n)).wait_recv())
    total = lax.fori_loop(0, n, lambda i, t: t + loss_seq[i], jnp.zeros((8, 128), F32))
    loss_ref[...] = jnp.broadcast_to(jnp.sum(total) * inv_total, (8, 128))

    def unpack(src, dst):
        for h in range(half):
            x = src[h * 128 : (h + 1) * 128]
            dst[h] = x[:, 0:64]
            dst[h + half] = pltpu.roll(x, 64, 1)[:, 0:64]

    q_total.finish()
    unpack(aq_out, gq_ref)
    k_total.finish()
    unpack(ak_out, gk_ref)

    fwd.drain()
    bwd.drain()
    q_total.drain()
    k_total.drain()

    @pl.when(me < n - 1)
    def _():
        edge_copy(0, me + 1).wait_send()
        edge_copy(1, me + 1).wait_send()

    peers(m, lambda i: loss_cols(lax.rem(col + i, m), col).wait_send())
    peers(n, lambda i: loss_rows(lax.rem(me + i, n), me).wait_send())


def body(queries, keys, values, teacher, q_map, k_map):
    tok, heads, width = queries.shape
    n, m = lax.axis_size("seq"), lax.axis_size("kvh")
    nblk = tok // BLK
    vmem = lambda shape, dtype=F32: pltpu.VMEM(shape, dtype)
    dma = lambda *shape: pltpu.SemaphoreType.DMA(shape)
    state = heads * 128
    grad = heads * 64
    scan_bufs = lambda: [
        vmem((state, 128)),
        vmem((8, 128)),
        vmem((n, state // n, 128)),
        vmem((n, state // n, 128)),
        vmem((state, 128)),
        vmem((n, 8, 128)),
        vmem((n, 8, 128)),
        vmem((8, 128)),
    ]
    total_bufs = lambda: [vmem((grad, 128)), vmem((n, grad // n, 128)), vmem((grad // n, 128)), vmem((grad, 128))]
    spec = pl.BlockSpec(memory_space=pltpu.VMEM)
    outs, grad_q, grad_k, loss = pl.pallas_call(
        functools.partial(kernel, n, m, heads, tok, width**-0.5, 1.0 / (tok * n)),
        out_shape=(
            jax.ShapeDtypeStruct((tok * heads, width), BF16),
            jax.ShapeDtypeStruct(q_map.shape, F32),
            jax.ShapeDtypeStruct(k_map.shape, F32),
            jax.ShapeDtypeStruct((8, 128), F32),
        ),
        in_specs=[spec] * 6,
        out_specs=(spec,) * 4,
        scratch_shapes=[
            vmem((tok * heads, width)),
            vmem((tok + 2 * WIN, 128), BF16),
            vmem((tok + 2 * WIN, 128), BF16),
            vmem((tok + 2 * WIN, 256), BF16),
            vmem((256, tok), BF16),
            vmem((128, tok), BF16),
            vmem((heads, tok, 128), BF16),
            vmem((heads, tok, 128), BF16),
            vmem((heads, tok, 128), BF16),
            vmem((heads, tok + WIN, 128), BF16),
            vmem((heads, tok + WIN, 128), BF16),
            *scan_bufs(),
            vmem((heads, nblk, 128, 128)),
            vmem((heads, nblk, 8, 128)),
            vmem((heads, tok, 256)),
            vmem((heads, tok, 128)),
            vmem((heads, tok, 128)),
            vmem((heads, nblk, 128, 128)),
            vmem((heads, nblk, 8, 128)),
            *scan_bufs(),
            vmem((heads, tok, 128)),
            *total_bufs(),
            *total_bufs(),
            vmem((8, 128)),
            vmem((m, 8, 128)),
            vmem((8, 128)),
            vmem((n, 8, 128)),
            dma(4, n),
            dma(3, n),
            dma(4, n),
            dma(3, n),
            dma(4, n),
            dma(4, n),
            dma(2, 2),
            dma(2, m),
            dma(2, n),
        ],
        compiler_params=pltpu.CompilerParams(collective_id=1, has_side_effects=True, vmem_limit_bytes=58 << 20),
    )(
        queries.reshape(tok * heads, width),
        keys.reshape(tok, width),
        values.reshape(tok, width),
        teacher.reshape(tok * heads, width),
        q_map,
        k_map,
    )
    return outs.reshape(tok, heads, width), grad_q, grad_k, loss[0, 0]


def solution(mesh):
    in_specs = (
        P("seq", "kvh", None),
        P("seq", "kvh", None),
        P("seq", "kvh", None),
        P("seq", "kvh", None),
        P("kvh", None, None),
        P("kvh", None, None),
    )
    out_specs = (P("seq", "kvh", None), P("kvh", None, None), P("kvh", None, None), P())
    return jax.shard_map(body, mesh=mesh, in_specs=in_specs, out_specs=out_specs, check_vma=False)
```

```python
import functools

import jax
import jax.numpy as jnp
from jax import lax
from jax.experimental import pallas as pl
from jax.experimental.pallas import tpu as pltpu
from jax.sharding import PartitionSpec as P

WIN = 64
BLK = 128
F32, BF16 = jnp.float32, jnp.bfloat16
MESH = pl.DeviceIdType.MESH


def split(x):
    hi = x.astype(BF16)
    return hi, (x - hi.astype(F32)).astype(BF16)


def nn(a, b):
    return lax.dot_general(a, b, (((1,), (0,)), ((), ())), preferred_element_type=F32)


def nt(a, b):
    return lax.dot_general(a, b, (((1,), (1,)), ((), ())), preferred_element_type=F32)


def lanes(*parts):
    return jnp.concatenate(parts, axis=1)


def rows(*parts):
    return jnp.concatenate(parts, axis=0)


def peers(n, fn):
    def go(i, carry):
        fn(i)
        return carry

    lax.fori_loop(1, n, go, 0)


def remote(src, dst, send, recv, dev, axis="seq"):
    return pltpu.make_async_remote_copy(
        src_ref=src, dst_ref=dst, send_sem=send, recv_sem=recv, device_id={axis: dev}, device_id_type=MESH
    )


class Scan:
    def __init__(self, n, me, own, own_norm, got, part, out, got_norm, part_norm, out_norm, sems, norm_sems, reverse):
        self.__dict__.update(locals())
        self.chunk = own.shape[0] // n
        self.keeper = n // 2

    def piece(self, dev):
        return pl.ds(pl.multiple_of(dev * self.chunk, 8), self.chunk)

    def next(self):
        return lax.rem(self.me + 1, self.n)

    def first(self, dev):
        return remote(self.own.at[self.piece(dev)], self.got.at[self.me], self.sems.at[0], self.sems.at[1], dev)

    def second(self, dev):
        return remote(self.part.at[dev], self.out.at[self.piece(self.me)], self.sems.at[2], self.sems.at[3], dev)

    def all_first(self):
        block = self.got.at[pl.ds(0, self.n - 1)]
        return remote(block, block, self.sems.at[0], self.sems.at[1], self.next())

    def all_second(self):
        block = self.out.at[pl.ds(0, (self.n - 1) * self.chunk)]
        return remote(block, block, self.sems.at[2], self.sems.at[3], self.next())

    def norm_first(self):
        return remote(self.own_norm, self.got_norm.at[self.me], self.norm_sems.at[0], self.norm_sems.at[1], self.keeper)

    def norm_second(self, dev):
        return remote(self.part_norm.at[dev], self.out_norm, self.norm_sems.at[2], self.norm_sems.at[3], dev)

    def all_norms(self):
        block = self.got_norm.at[pl.ds(0, self.n - 1)]
        return remote(block, block, self.norm_sems.at[2], self.norm_sems.at[1], self.next())

    def start(self):
        n, me = self.n, self.me
        peers(n, lambda i: self.first(lax.rem(me + i, n)).start())

        @pl.when(me != self.keeper)
        def _():
            self.norm_first().start()

    def sums(self, got, part, zero):
        n = self.n

        def go(i, total):
            at = n - 1 - i if self.reverse else i
            part[at] = total
            return total + got[at]

        return lax.fori_loop(0, n, go, zero)

    def turn(self):
        n, me, keeper = self.n, self.me, self.keeper
        self.got[me] = self.own[self.piece(me)]
        self.all_first().wait_recv()
        self.sums(self.got, self.part, jnp.zeros((self.chunk, 128), F32))
        peers(n, lambda i: self.second(lax.rem(me + i, n)).start())
        self.out[self.piece(me)] = self.part[me]

        @pl.when(me == keeper)
        def _():
            self.got_norm[keeper] = self.own_norm[...]
            self.all_norms().wait_recv()
            total = self.sums(self.got_norm, self.part_norm, jnp.zeros((16, 128), F32))
            self.part_norm[:, 8:16] = jnp.broadcast_to(total[None, 8:16], (n, 8, 128))
            peers(n, lambda i: self.norm_second(lax.rem(keeper + i, n)).start())
            self.out_norm[...] = self.part_norm[keeper]

    def finish(self):
        self.all_second().wait_recv()

        @pl.when(self.me != self.keeper)
        def _():
            self.norm_second(self.next()).wait_recv()

    def drain(self):
        self.all_first().wait_send()
        self.all_second().wait_send()

        @pl.when(self.me != self.keeper)
        def _():
            self.norm_first().wait_send()

        @pl.when(self.me == self.keeper)
        def _():
            self.all_norms().wait_send()


class Total:
    def __init__(self, n, me, own, got, part, out, sems):
        self.__dict__.update(locals())
        self.chunk = own.shape[0] // n

    def piece(self, dev):
        return pl.ds(pl.multiple_of(dev * self.chunk, 8), self.chunk)

    def next(self):
        return lax.rem(self.me + 1, self.n)

    def first(self, dev):
        return remote(self.own.at[self.piece(dev)], self.got.at[self.me], self.sems.at[0], self.sems.at[1], dev)

    def second(self, dev):
        return remote(self.part, self.out.at[self.piece(self.me)], self.sems.at[2], self.sems.at[3], dev)

    def all_first(self):
        block = self.got.at[pl.ds(0, self.n - 1)]
        return remote(block, block, self.sems.at[0], self.sems.at[1], self.next())

    def all_second(self):
        block = self.out.at[pl.ds(0, (self.n - 1) * self.chunk)]
        return remote(block, block, self.sems.at[2], self.sems.at[3], self.next())

    def start(self):
        peers(self.n, lambda i: self.first(lax.rem(self.me + i, self.n)).start())

    def turn(self):
        n, me = self.n, self.me
        self.got[me] = self.own[self.piece(me)]
        self.all_first().wait_recv()
        self.part[...] = lax.fori_loop(0, n, lambda i, t: t + self.got[i], jnp.zeros((self.chunk, 128), F32))
        peers(n, lambda i: self.second(lax.rem(me + i, n)).start())
        self.out[self.piece(me)] = self.part[...]

    def finish(self):
        self.all_second().wait_recv()

    def drain(self):
        self.all_first().wait_send()
        self.all_second().wait_send()


def each(lo, hi, fn, init=0, unroll=2):
    def go(i, carry):
        for u in range(unroll):
            carry = fn(lo + i * unroll + u, carry)
        return carry

    return lax.fori_loop(0, (hi - lo) // unroll, go, init)


def kernel(n, m, heads, tok, scale, inv_total, q_hbm, k_ref, v_ref, t_hbm, wq_ref, wk_ref,
           y_hbm, gq_ref, gk_ref, loss_ref,
           tmp, kext, vext, vaug, vaugt, kt, qh, pqh, pql, pkh, pkl,
           s_own, s_norm, s_got, s_part, s_in, sn_got, sn_part, sn_in,
           loc, loc_norm, numer, gn_s, gd_s, dblk, dblk_norm,
           d_own, d_norm, d_got, d_part, d_in, dn_got, dn_part, dn_in,
           gkf, aq, aq_got, aq_part, aq_out, ak, ak_got, ak_part, ak_out,
           loss_row, loss_kv, q_ref, t_ref, y_ref,
           f_sems, fn_sems, b_sems, bn_sems, q_sems, k_sems, e_sems, lk_sems, io_sems):
    me = lax.axis_index("seq")
    col = lax.axis_index("kvh")
    nblk = tok // BLK

    barrier = pltpu.get_barrier_semaphore()
    peers(n, lambda i: pl.semaphore_signal(barrier, inc=1, device_id={"seq": lax.rem(me + i, n)}, device_id_type=MESH))
    peers(m, lambda i: pl.semaphore_signal(barrier, inc=1, device_id={"kvh": lax.rem(col + i, m)}, device_id_type=MESH))
    load_q = pltpu.make_async_copy(q_hbm, q_ref, io_sems.at[0])
    load_t = pltpu.make_async_copy(t_hbm, t_ref, io_sems.at[1])
    save_y = pltpu.make_async_copy(y_ref, y_hbm, io_sems.at[2])
    load_q.start()
    load_t.start()

    lane = lax.broadcasted_iota(jnp.int32, (1, 128), 1)
    upper = lane < 64
    ri = lax.broadcasted_iota(jnp.int32, (256, 128), 0)
    ci = lax.broadcasted_iota(jnp.int32, (256, 128), 1)
    ones2 = jnp.where((lax.rem(ri, 128) < 64) == (ci < 64), 1.0, 0.0).astype(BF16)

    def half_sums(x):
        hi, lo = split(x)
        return nn(lanes(hi, lo), ones2)

    def maps(x, w):
        w = w.astype(F32)
        a = nt(x, rows(w, -w).astype(BF16))
        low = jnp.full_like(a, -jnp.inf)
        top = jnp.where(
            upper,
            jnp.max(jnp.where(upper, a, low), axis=-1, keepdims=True),
            jnp.max(jnp.where(upper, low, a), axis=-1, keepdims=True),
        )
        e = jnp.exp(a - top)
        return e / half_sums(e)

    def back(phi, g):
        return phi * (g - half_sums(phi * g))

    kext[WIN : WIN + tok] = k_ref[...]
    vext[WIN : WIN + tok] = v_ref[...]
    vt = v_ref[...].astype(F32).T.astype(BF16)
    vt2 = lanes(vt, vt)

    def own_keys(h, carry):
        phi = maps(k_ref[...], wk_ref[h])
        hi, lo = split(phi)
        pkh[h, WIN : WIN + tok] = hi
        pkl[h, WIN : WIN + tok] = lo
        s_own[pl.ds(pl.multiple_of(h * 128, 128), 128)] = nn(vt2, rows(hi, lo))
        s_norm[pl.ds(h, 1)] = jnp.sum(phi, axis=0, keepdims=True)
        return carry

    each(0, heads, own_keys)
    s_norm[8:16] = jnp.zeros((8, 128), F32)
    pl.semaphore_wait(barrier, n - 1 + m - 1)

    def edge_copy(i, dev):
        src, dst = (k_ref, kext) if i == 0 else (v_ref, vext)
        return remote(src.at[pl.ds(tok - WIN, WIN)], dst.at[pl.ds(0, WIN)], e_sems.at[0, i], e_sems.at[1, i], dev)

    @pl.when(me < n - 1)
    def _():
        edge_copy(0, me + 1).start()
        edge_copy(1, me + 1).start()

    fwd = Scan(n, me, s_own, s_norm, s_got, s_part, s_in, sn_got, sn_part, sn_in, f_sems, fn_sems, False)
    bwd = Scan(n, me, d_own, d_norm, d_got, d_part, d_in, dn_got, dn_part, dn_in, b_sems, bn_sems, True)
    fwd.start()

    load_q.wait()
    tmp[...] = q_ref[...].astype(F32)

    def query_maps(h, carry):
        x = tmp[pl.ds(h, tok, stride=heads), :].astype(BF16)
        qh[h] = x
        hi, lo = split(maps(x, wq_ref[h]))
        pqh[h] = hi
        pql[h] = lo
        return carry

    each(0, heads, query_maps)

    @pl.when(me == 0)
    def _():
        kext[0:WIN] = jnp.zeros((WIN, 128), BF16)
        vext[0:WIN] = jnp.zeros((WIN, 128), BF16)

    @pl.when(me > 0)
    def _():
        edge_copy(0, me - 1).wait_recv()
        edge_copy(1, me - 1).wait_recv()

    pad = jnp.zeros((WIN, 128), BF16)
    kext[WIN + tok :] = pad
    vext[WIN + tok :] = pad
    valid = jnp.where(me > 0, 1.0, 0.0).astype(F32)
    vaug[:, 0:128] = vext[...]
    vaug[:, 128:256] = jnp.ones((tok + 2 * WIN, 128), BF16)
    vaugt[0:128] = vext[0:tok].astype(F32).T.astype(BF16)
    vaugt[128:256] = jnp.ones((128, tok), BF16)
    kt[...] = kext[0:tok].astype(F32).T.astype(BF16)

    def edge_maps(h, carry):
        phi = maps(kext[0:WIN], wk_ref[h]) * valid
        hi, lo = split(phi)
        pkh[h, 0:WIN] = hi
        pkl[h, 0:WIN] = lo
        return carry

    each(0, heads, edge_maps)

    r2 = lax.broadcasted_iota(jnp.int32, (BLK, 2 * BLK), 0)
    c2 = lax.broadcasted_iota(jnp.int32, (BLK, 2 * BLK), 1)
    near_band = (c2 > r2) & (c2 <= r2 + WIN)
    first_key = jnp.where(me > 0, 0, WIN)
    r1 = lax.broadcasted_iota(jnp.int32, (BLK, BLK), 0)
    c1 = lax.broadcasted_iota(jnp.int32, (BLK, BLK), 1)
    causal = c1 <= r1

    def local_forward(h, carry):
        ph0 = pkh[h, 0:WIN]
        pl0 = pkl[h, 0:WIN]
        zero = jnp.zeros((WIN, 128), BF16)
        vb = vaugt[:, 0:BLK]
        state = -nn(lanes(vb, vb), rows(ph0, zero, pl0, zero))
        for b in range(nblk):
            at = b * BLK
            loc[h, b] = state[0:128]
            loc_norm[h, b] = state[128:136]
            kh = pkh[h, at : at + BLK]
            kl = pkl[h, at : at + BLK]
            qhi = pqh[h, at : at + BLK]
            qlo = pql[h, at : at + BLK]
            q3 = lanes(qhi, qlo, qhi)
            far = jnp.where(causal, nt(q3, lanes(kh, kh, kl)), 0.0)
            s = nt(qh[h, at : at + BLK], kext[at : at + 2 * BLK]) * scale
            mask = near_band & (c2 >= first_key) if b == 0 else near_band
            s = jnp.where(mask, s, -1e30)
            top = jnp.max(s, axis=-1, keepdims=True)
            w = jnp.where(mask, jnp.exp(s - top), 0.0)
            w = lanes(w[:, 0:BLK] + far, w[:, BLK:])
            whi, wlo = split(w)
            va = vaug[at : at + 2 * BLK]
            shi, slo = split(state)
            numer[h, at : at + BLK] = nn(lanes(whi, wlo), rows(va, va)) + nt(q3, lanes(shi, shi, slo))
            if b + 1 < nblk:
                vb = vaugt[:, at : at + BLK]
                state = state + nn(lanes(vb, vb), rows(kh, kl))
        return carry

    each(0, heads // 2, local_forward)
    fwd.turn()
    each(heads // 2, heads, local_forward)
    fwd.finish()

    load_t.wait()
    tmp[...] = t_ref[...].astype(F32)

    def outputs(h, squares):
        prior = s_in[pl.ds(pl.multiple_of(h * 128, 128), 128)]
        prior_norm = jnp.broadcast_to(sn_in[pl.ds(h, 1)], (128, 128))
        shi, slo = split(rows(prior, prior_norm))
        s3 = lanes(shi, shi, slo)
        d_sum = jnp.zeros((128, 128), F32)
        dn_sum = jnp.zeros((1, 128), F32)
        for b in range(nblk):
            at = b * BLK
            qhi = pqh[h, at : at + BLK]
            qlo = pql[h, at : at + BLK]
            both = numer[h, at : at + BLK] + nt(lanes(qhi, qlo, qhi), s3)
            den = both[:, 128:256]
            y = both[:, 0:128] / den
            where = pl.ds(h + at * heads, BLK, stride=heads)
            error = y - tmp[where, :]
            tmp[where, :] = y
            squares = squares + jnp.sum((error * error).reshape(BLK // 8, 8, 128), axis=0)
            gn = (2.0 * inv_total) * error / den
            gd = jnp.broadcast_to(-jnp.sum(gn * y, axis=-1, keepdims=True), (BLK, 128))
            gn_s[h, at : at + BLK] = gn
            gd_s[h, at : at + BLK] = gd
            ghi, glo = split(gn.T)
            d = nn(lanes(ghi, glo, ghi), rows(qhi, qhi, qlo))
            dn = jnp.sum(gd * (qhi.astype(F32) + qlo.astype(F32)), axis=0, keepdims=True)
            dblk[h, b] = d
            dblk_norm[h, b] = jnp.broadcast_to(dn, (8, 128))
            d_sum = d_sum + d
            dn_sum = dn_sum + dn
        d_own[pl.ds(pl.multiple_of(h * 128, 128), 128)] = d_sum
        d_norm[pl.ds(h, 1)] = dn_sum
        return squares

    d_norm[8:16] = each(0, heads, outputs, jnp.zeros((8, 128), F32))
    bwd.start()

    def loss_cols(dev, src):
        return remote(loss_row, loss_kv.at[src], lk_sems.at[0, dev], lk_sems.at[1, src], dev, "kvh")

    y_ref[...] = tmp[...].astype(BF16)
    save_y.start()

    def local_backward(h, carry):
        prior = s_in[pl.ds(pl.multiple_of(h * 128, 128), 128)]
        prior_norm = sn_in[pl.ds(h, 1)]
        later = jnp.zeros((128, 128), F32)
        later_norm = jnp.zeros((1, 128), F32)
        g = jnp.zeros((128, 128), F32)
        for b in reversed(range(nblk)):
            at = b * BLK
            gn = gn_s[h, at : at + BLK]
            gd = gd_s[h, at : at + BLK]
            vb = vext[at : at + BLK]
            kh = pkh[h, at : at + BLK]
            kl = pkl[h, at : at + BLK]
            qhi = pqh[h, at : at + BLK]
            qlo = pql[h, at : at + BLK]
            ghi, glo = split(gn)
            gf = jnp.where(causal, nt(lanes(ghi, glo), lanes(vb, vb)) + gd, 0.0)
            fhi, flo = split(gf)
            shi, slo = split(prior + loc[h, b])
            norm = prior_norm + loc_norm[h, b, 0:1]
            gqf = nn(lanes(fhi, flo, fhi, ghi, glo, ghi), rows(kh, kh, kl, shi, shi, slo)) + gd * norm
            rhi, rlo = split(back(qhi.astype(F32) + qlo.astype(F32), gqf))
            qt = qh[h, at : at + BLK].astype(F32).T.astype(BF16)
            g = g + nn(lanes(qt, qt), rows(rhi, rlo))
            thi, tlo = split(gf.T)
            lhi, llo = split(later)
            gkf[h, at : at + BLK] = (
                nn(lanes(thi, tlo, thi, vb, vb), rows(qhi, qhi, qlo, lhi, llo)) + later_norm
            )
            later = later + dblk[h, b]
            later_norm = later_norm + dblk_norm[h, b, 0:1]
        put(aq, h, g)
        return carry

    def put(ref, h, g):
        g = g.T
        ref[pl.ds(pl.multiple_of(h * 64, 64), 64)] = g[0:64] - g[64:128]

    each(0, heads // 2, local_backward)
    bwd.turn()
    each(heads // 2, heads, local_backward)
    q_total = Total(n, me, aq, aq_got, aq_part, aq_out, q_sems)
    k_total = Total(n, me, ak, ak_got, ak_part, ak_out, k_sems)
    q_total.start()
    bwd.finish()
    loss_row[...] = dn_in[8:16]
    peers(m, lambda i: loss_cols(lax.rem(col + i, m), col).start())

    def key_grads(h, carry):
        shi, slo = split(d_in[pl.ds(pl.multiple_of(h * 128, 128), 128)])
        suffix_norm = dn_in[pl.ds(h, 1)]
        v = vext[0:tok]
        g = gkf[h] + nn(lanes(v, v), rows(shi, slo)) + suffix_norm
        hi, lo = split(back(pkh[h, 0:tok].astype(F32) + pkl[h, 0:tok].astype(F32), g))
        t = kt[...]
        put(ak, h, nn(lanes(t, t), rows(hi, lo)))
        return carry

    each(0, heads, key_grads)
    k_total.start()
    q_total.turn()
    k_total.turn()

    loss_kv[col] = loss_row[...]
    peers(m, lambda i: loss_cols(col, lax.rem(col + i, m)).wait_recv())
    total = lax.fori_loop(0, m, lambda i, t: t + loss_kv[i], jnp.zeros((8, 128), F32))
    loss_ref[0, 0] = jnp.sum(total) * inv_total

    q_total.finish()
    gq_ref[...] = aq_out[...]

    fwd.drain()
    bwd.drain()

    @pl.when(me < n - 1)
    def _():
        edge_copy(0, me + 1).wait_send()
        edge_copy(1, me + 1).wait_send()

    peers(m, lambda i: loss_cols(lax.rem(col + i, m), col).wait_send())
    save_y.wait()
    k_total.finish()
    gk_ref[...] = ak_out[...]
    q_total.drain()
    k_total.drain()


def body(queries, keys, values, teacher, q_map, k_map):
    tok, heads, width = queries.shape
    n, m = lax.axis_size("seq"), lax.axis_size("kvh")
    nblk = tok // BLK
    vmem = lambda shape, dtype=F32: pltpu.VMEM(shape, dtype)
    dma = lambda *shape: pltpu.SemaphoreType.DMA(shape)
    state = heads * 128
    grad = heads * 64
    scan_bufs = lambda: [
        vmem((state, 128)),
        vmem((16, 128)),
        vmem((n, state // n, 128)),
        vmem((n, state // n, 128)),
        vmem((state, 128)),
        vmem((n, 16, 128)),
        vmem((n, 16, 128)),
        vmem((16, 128)),
    ]
    total_bufs = lambda: [vmem((grad, 128)), vmem((n, grad // n, 128)), vmem((grad // n, 128)), vmem((grad, 128))]
    spec = pl.BlockSpec(memory_space=pltpu.VMEM)
    hbm = pl.BlockSpec(memory_space=pl.ANY)
    outs, grad_q, grad_k, loss = pl.pallas_call(
        functools.partial(kernel, n, m, heads, tok, width**-0.5, 1.0 / (tok * n)),
        out_shape=(
            jax.ShapeDtypeStruct((tok * heads, width), BF16),
            jax.ShapeDtypeStruct((grad, width), F32),
            jax.ShapeDtypeStruct((grad, width), F32),
            jax.ShapeDtypeStruct((1, 1), F32),
        ),
        in_specs=[hbm, spec, spec, hbm, spec, spec],
        out_specs=(hbm, spec, spec, pl.BlockSpec(memory_space=pltpu.SMEM)),
        scratch_shapes=[
            vmem((tok * heads, width)),
            vmem((tok + 2 * WIN, 128), BF16),
            vmem((tok + 2 * WIN, 128), BF16),
            vmem((tok + 2 * WIN, 256), BF16),
            vmem((256, tok), BF16),
            vmem((128, tok), BF16),
            vmem((heads, tok, 128), BF16),
            vmem((heads, tok, 128), BF16),
            vmem((heads, tok, 128), BF16),
            vmem((heads, tok + WIN, 128), BF16),
            vmem((heads, tok + WIN, 128), BF16),
            *scan_bufs(),
            vmem((heads, nblk, 128, 128)),
            vmem((heads, nblk, 8, 128)),
            vmem((heads, tok, 256)),
            vmem((heads, tok, 128)),
            vmem((heads, tok, 128)),
            vmem((heads, nblk, 128, 128)),
            vmem((heads, nblk, 8, 128)),
            *scan_bufs(),
            vmem((heads, tok, 128)),
            *total_bufs(),
            *total_bufs(),
            vmem((8, 128)),
            vmem((m, 8, 128)),
            vmem((tok * heads, width), BF16),
            vmem((tok * heads, width), BF16),
            vmem((tok * heads, width), BF16),
            dma(4),
            dma(4),
            dma(4),
            dma(4),
            dma(4),
            dma(4),
            dma(2, 2),
            dma(2, m),
            dma(3),
        ],
        compiler_params=pltpu.CompilerParams(collective_id=1, has_side_effects=True, vmem_limit_bytes=58 << 20),
    )(
        queries.reshape(tok * heads, width),
        keys.reshape(tok, width),
        values.reshape(tok, width),
        teacher.reshape(tok * heads, width),
        jnp.swapaxes(q_map, 1, 2),
        jnp.swapaxes(k_map, 1, 2),
    )
    unmap = lambda g: jnp.swapaxes(g.reshape(heads, 64, width), 1, 2)
    return outs.reshape(tok, heads, width), unmap(grad_q), unmap(grad_k), loss.reshape(())


def solution(mesh):
    in_specs = (
        P("seq", "kvh", None),
        P("seq", "kvh", None),
        P("seq", "kvh", None),
        P("seq", "kvh", None),
        P("kvh", None, None),
        P("kvh", None, None),
    )
    out_specs = (P("seq", "kvh", None), P("kvh", None, None), P("kvh", None, None), P())
    return jax.shard_map(body, mesh=mesh, in_specs=in_specs, out_specs=out_specs, check_vma=False)
```

```python
import functools

import jax
import jax.numpy as jnp
from jax import lax
from jax.experimental import pallas as pl
from jax.experimental.pallas import tpu as pltpu
from jax.sharding import PartitionSpec as P

WIN = 64
BLK = 128
F32, BF16 = jnp.float32, jnp.bfloat16
MESH = pl.DeviceIdType.MESH


def split(x):
    hi = x.astype(BF16)
    return hi, (x - hi.astype(F32)).astype(BF16)


def nn(a, b):
    return lax.dot_general(a, b, (((1,), (0,)), ((), ())), preferred_element_type=F32)


def nt(a, b):
    return lax.dot_general(a, b, (((1,), (1,)), ((), ())), preferred_element_type=F32)


def lanes(*parts):
    return jnp.concatenate(parts, axis=1)


def rows(*parts):
    return jnp.concatenate(parts, axis=0)


def peers(n, fn):
    def go(i, carry):
        fn(i)
        return carry

    lax.fori_loop(1, n, go, 0)


def remote(src, dst, send, recv, dev, axis="seq"):
    return pltpu.make_async_remote_copy(
        src_ref=src, dst_ref=dst, send_sem=send, recv_sem=recv, device_id={axis: dev}, device_id_type=MESH
    )


class Scan:
    def __init__(self, n, me, own, own_norm, got, part, out, got_norm, part_norm, out_norm, sems, norm_sems, reverse, keeper):
        self.__dict__.update(locals())
        self.chunk = own.shape[0] // n

    def piece(self, dev):
        return pl.ds(pl.multiple_of(dev * self.chunk, 8), self.chunk)

    def next(self):
        return lax.rem(self.me + 1, self.n)

    def first(self, dev):
        return remote(self.own.at[self.piece(dev)], self.got.at[self.me], self.sems.at[0], self.sems.at[1], dev)

    def second(self, dev):
        return remote(self.part.at[dev], self.out.at[self.piece(self.me)], self.sems.at[2], self.sems.at[3], dev)

    def all_first(self):
        block = self.got.at[pl.ds(0, self.n - 1)]
        return remote(block, block, self.sems.at[0], self.sems.at[1], self.next())

    def all_second(self):
        block = self.out.at[pl.ds(0, (self.n - 1) * self.chunk)]
        return remote(block, block, self.sems.at[2], self.sems.at[3], self.next())

    def norm_first(self):
        return remote(self.own_norm, self.got_norm.at[self.me], self.norm_sems.at[0], self.norm_sems.at[1], self.keeper)

    def norm_second(self, dev):
        return remote(self.part_norm.at[dev], self.out_norm, self.norm_sems.at[2], self.norm_sems.at[3], dev)

    def all_norms(self):
        block = self.got_norm.at[pl.ds(0, self.n - 1)]
        return remote(block, block, self.norm_sems.at[2], self.norm_sems.at[1], self.next())

    def start(self):
        n, me = self.n, self.me
        peers(n, lambda i: self.first(lax.rem(me + i, n)).start())

        @pl.when(me != self.keeper)
        def _():
            self.norm_first().start()

    def sums(self, got, part, zero):
        n = self.n

        def go(i, total):
            at = n - 1 - i if self.reverse else i
            part[at] = total
            return total + got[at]

        return lax.fori_loop(0, n, go, zero)

    def turn(self):
        n, me, keeper = self.n, self.me, self.keeper
        self.got[me] = self.own[self.piece(me)]
        self.all_first().wait_recv()
        self.sums(self.got, self.part, jnp.zeros((self.chunk, 128), F32))
        peers(n, lambda i: self.second(lax.rem(me + i, n)).start())
        self.out[self.piece(me)] = self.part[me]

        @pl.when(me == keeper)
        def _():
            self.got_norm[keeper] = self.own_norm[...]
            self.all_norms().wait_recv()
            total = self.sums(self.got_norm, self.part_norm, jnp.zeros((16, 128), F32))
            self.part_norm[:, 8:16] = jnp.broadcast_to(total[None, 8:16], (n, 8, 128))
            peers(n, lambda i: self.norm_second(lax.rem(keeper + i, n)).start())
            self.out_norm[...] = self.part_norm[keeper]

    def finish(self):
        self.all_second().wait_recv()

        @pl.when(self.me != self.keeper)
        def _():
            self.norm_second(self.next()).wait_recv()

    def drain(self):
        self.all_first().wait_send()
        self.all_second().wait_send()

        @pl.when(self.me != self.keeper)
        def _():
            self.norm_first().wait_send()

        @pl.when(self.me == self.keeper)
        def _():
            self.all_norms().wait_send()


class Total:
    def __init__(self, n, me, own, got, part, out, sems):
        self.__dict__.update(locals())
        self.chunk = own.shape[0] // n

    def piece(self, dev):
        return pl.ds(pl.multiple_of(dev * self.chunk, 8), self.chunk)

    def next(self):
        return lax.rem(self.me + 1, self.n)

    def first(self, dev):
        return remote(self.own.at[self.piece(dev)], self.got.at[self.me], self.sems.at[0], self.sems.at[1], dev)

    def second(self, dev):
        return remote(self.part, self.out.at[self.piece(self.me)], self.sems.at[2], self.sems.at[3], dev)

    def all_first(self):
        block = self.got.at[pl.ds(0, self.n - 1)]
        return remote(block, block, self.sems.at[0], self.sems.at[1], self.next())

    def all_second(self):
        block = self.out.at[pl.ds(0, (self.n - 1) * self.chunk)]
        return remote(block, block, self.sems.at[2], self.sems.at[3], self.next())

    def start(self):
        peers(self.n, lambda i: self.first(lax.rem(self.me + i, self.n)).start())

    def turn(self):
        n, me = self.n, self.me
        self.got[me] = self.own[self.piece(me)]
        self.all_first().wait_recv()
        self.part[...] = lax.fori_loop(0, n, lambda i, t: t + self.got[i], jnp.zeros((self.chunk, 128), F32))
        peers(n, lambda i: self.second(lax.rem(me + i, n)).start())
        self.out[self.piece(me)] = self.part[...]

    def finish(self):
        self.all_second().wait_recv()

    def drain(self):
        self.all_first().wait_send()
        self.all_second().wait_send()


def each(lo, hi, fn, init=0, unroll=2):
    def go(i, carry):
        for u in range(unroll):
            carry = fn(lo + i * unroll + u, carry)
        return carry

    return lax.fori_loop(0, (hi - lo) // unroll, go, init)


def kernel(n, m, heads, tok, scale, inv_total, q_hbm, k_ref, v_ref, t_hbm, wq_ref, wk_ref,
           y_hbm, gq_ref, gk_ref, loss_ref,
           tmp, kext, vext, vaug, vaugt, kt, qh, qt, pqh, pql, pkh, pkl,
           bufs_fa, bufs_fb,
           loc, loc_norm, numer, gn_s, gd_s, dblk, dblk_norm,
           bufs_ba, bufs_bb,
           gkf, aq, aq_got, aq_part, aq_out, ak, ak_got, ak_part, ak_out,
           loss_row, loss_kv, q_ref, t_ref, y_ref,
           sems_fa, sems_fb, sems_ba, sems_bb, q_sems, k_sems, e_sems, lk_sems, io_sems):
    me = lax.axis_index("seq")
    col = lax.axis_index("kvh")
    nblk = tok // BLK
    half = heads // 2

    barrier = pltpu.get_barrier_semaphore()
    peers(n, lambda i: pl.semaphore_signal(barrier, inc=1, device_id={"seq": lax.rem(me + i, n)}, device_id_type=MESH))
    peers(m, lambda i: pl.semaphore_signal(barrier, inc=1, device_id={"kvh": lax.rem(col + i, m)}, device_id_type=MESH))
    load_q = pltpu.make_async_copy(q_hbm, q_ref, io_sems.at[0])
    load_t = pltpu.make_async_copy(t_hbm, t_ref, io_sems.at[1])
    save_y = pltpu.make_async_copy(y_ref, y_hbm, io_sems.at[2])
    load_q.start()
    load_t.start()

    lane = lax.broadcasted_iota(jnp.int32, (1, 128), 1)
    upper = lane < 64
    ri = lax.broadcasted_iota(jnp.int32, (256, 128), 0)
    ci = lax.broadcasted_iota(jnp.int32, (256, 128), 1)
    ones2 = jnp.where((lax.rem(ri, 128) < 64) == (ci < 64), 1.0, 0.0).astype(BF16)

    def half_sums(x):
        hi, lo = split(x)
        return nn(lanes(hi, lo), ones2)

    def maps(x, w):
        w = w.astype(F32)
        a = nt(x, rows(w, -w).astype(BF16))
        low = jnp.full_like(a, -jnp.inf)
        top = jnp.where(
            upper,
            jnp.max(jnp.where(upper, a, low), axis=-1, keepdims=True),
            jnp.max(jnp.where(upper, low, a), axis=-1, keepdims=True),
        )
        e = jnp.exp(a - top)
        return e / half_sums(e)

    def back(phi, g):
        return phi * (g - half_sums(phi * g))

    fwd_a = Scan(n, me, *bufs_fa, *sems_fa, False, n // 2)
    fwd_b = Scan(n, me, *bufs_fb, *sems_fb, False, n // 2 - 1)
    bwd_a = Scan(n, me, *bufs_ba, *sems_ba, True, n // 2)
    bwd_b = Scan(n, me, *bufs_bb, *sems_bb, True, n // 2 - 1)

    def tile(h):
        return pl.ds(pl.multiple_of(lax.rem(h, half) * 128, 128), 128)

    def line(h):
        return pl.ds(lax.rem(h, half), 1)

    kext[WIN : WIN + tok] = k_ref[...]
    vext[WIN : WIN + tok] = v_ref[...]
    vt = v_ref[...].astype(F32).T.astype(BF16)
    vt2 = lanes(vt, vt)

    def own_keys(scan):
        def own_keys(h, carry):
            phi = maps(k_ref[...], wk_ref[h])
            hi, lo = split(phi)
            pkh[h, WIN : WIN + tok] = hi
            pkl[h, WIN : WIN + tok] = lo
            scan.own[tile(h)] = nn(vt2, rows(hi, lo))
            scan.own_norm[line(h)] = jnp.sum(phi, axis=0, keepdims=True)
            return carry

        return own_keys

    fwd_a.own_norm[...] = jnp.zeros((16, 128), F32)
    fwd_b.own_norm[...] = jnp.zeros((16, 128), F32)
    bwd_a.own_norm[...] = jnp.zeros((16, 128), F32)
    bwd_b.own_norm[...] = jnp.zeros((16, 128), F32)
    each(0, half, own_keys(fwd_a))
    each(half, heads, own_keys(fwd_b))

    load_q.wait()
    tmp[...] = q_ref[...].astype(F32)

    def query_maps(h, carry):
        f = tmp[pl.ds(h, tok, stride=heads), :]
        x = f.astype(BF16)
        qh[h] = x
        qt[h] = f.T.astype(BF16)
        hi, lo = split(maps(x, wq_ref[h]))
        pqh[h] = hi
        pql[h] = lo
        return carry

    each(0, heads, query_maps)
    pl.semaphore_wait(barrier, n - 1 + m - 1)

    def edge_copy(i, dev):
        src, dst = (k_ref, kext) if i == 0 else (v_ref, vext)
        return remote(src.at[pl.ds(tok - WIN, WIN)], dst.at[pl.ds(0, WIN)], e_sems.at[0, i], e_sems.at[1, i], dev)

    @pl.when(me < n - 1)
    def _():
        edge_copy(0, me + 1).start()
        edge_copy(1, me + 1).start()


    fwd_a.start()
    fwd_b.start()

    @pl.when(me == 0)
    def _():
        kext[0:WIN] = jnp.zeros((WIN, 128), BF16)
        vext[0:WIN] = jnp.zeros((WIN, 128), BF16)

    @pl.when(me > 0)
    def _():
        edge_copy(0, me - 1).wait_recv()
        edge_copy(1, me - 1).wait_recv()

    pad = jnp.zeros((WIN, 128), BF16)
    kext[WIN + tok :] = pad
    vext[WIN + tok :] = pad
    valid = jnp.where(me > 0, 1.0, 0.0).astype(F32)
    vaug[:, 0:128] = vext[...]
    vaug[:, 128:256] = jnp.ones((tok + 2 * WIN, 128), BF16)
    vaugt[0:128] = vext[0:tok].astype(F32).T.astype(BF16)
    vaugt[128:256] = jnp.ones((128, tok), BF16)
    kt[...] = kext[0:tok].astype(F32).T.astype(BF16)

    def edge_maps(h, carry):
        phi = maps(kext[0:WIN], wk_ref[h]) * valid
        hi, lo = split(phi)
        pkh[h, 0:WIN] = hi
        pkl[h, 0:WIN] = lo
        return carry

    each(0, heads, edge_maps)

    r2 = lax.broadcasted_iota(jnp.int32, (BLK, 2 * BLK), 0)
    c2 = lax.broadcasted_iota(jnp.int32, (BLK, 2 * BLK), 1)
    near_band = (c2 > r2) & (c2 <= r2 + WIN)
    first_key = jnp.where(me > 0, 0, WIN)
    r1 = lax.broadcasted_iota(jnp.int32, (BLK, BLK), 0)
    c1 = lax.broadcasted_iota(jnp.int32, (BLK, BLK), 1)
    causal = c1 <= r1

    def local_forward(h, carry):
        ph0 = pkh[h, 0:WIN]
        pl0 = pkl[h, 0:WIN]
        zero = jnp.zeros((WIN, 128), BF16)
        vb = vaugt[:, 0:BLK]
        state = -nn(lanes(vb, vb), rows(ph0, zero, pl0, zero))
        for b in range(nblk):
            at = b * BLK
            loc[h, b] = state[0:128]
            loc_norm[h, b] = state[128:136]
            kh = pkh[h, at : at + BLK]
            kl = pkl[h, at : at + BLK]
            qhi = pqh[h, at : at + BLK]
            qlo = pql[h, at : at + BLK]
            q3 = lanes(qhi, qlo, qhi)
            far = jnp.where(causal, nt(q3, lanes(kh, kh, kl)), 0.0)
            s = nt(qh[h, at : at + BLK], kext[at : at + 2 * BLK]) * scale
            mask = near_band & (c2 >= first_key) if b == 0 else near_band
            s = jnp.where(mask, s, -1e30)
            top = jnp.max(s, axis=-1, keepdims=True)
            w = jnp.where(mask, jnp.exp(s - top), 0.0)
            w = lanes(w[:, 0:BLK] + far, w[:, BLK:])
            whi, wlo = split(w)
            va = vaug[at : at + 2 * BLK]
            shi, slo = split(state)
            numer[h, at : at + BLK] = nn(lanes(whi, wlo), rows(va, va)) + nt(q3, lanes(shi, shi, slo))
            if b + 1 < nblk:
                vb = vaugt[:, at : at + BLK]
                state = state + nn(lanes(vb, vb), rows(kh, kl))
        return carry

    each(0, half, local_forward)
    fwd_a.turn()
    each(half, half + 2, local_forward)
    fwd_b.turn()
    each(half + 2, heads, local_forward)

    load_t.wait()
    tmp[...] = t_ref[...].astype(F32)

    def outputs(h, squares, fwd, bwd):
        prior = fwd.out[tile(h)]
        prior_norm = jnp.broadcast_to(fwd.out_norm[line(h)], (128, 128))
        shi, slo = split(rows(prior, prior_norm))
        s3 = lanes(shi, shi, slo)
        d_sum = jnp.zeros((128, 128), F32)
        dn_sum = jnp.zeros((1, 128), F32)
        for b in range(nblk):
            at = b * BLK
            qhi = pqh[h, at : at + BLK]
            qlo = pql[h, at : at + BLK]
            both = numer[h, at : at + BLK] + nt(lanes(qhi, qlo, qhi), s3)
            den = both[:, 128:256]
            y = both[:, 0:128] / den
            where = pl.ds(h + at * heads, BLK, stride=heads)
            error = y - tmp[where, :]
            tmp[where, :] = y
            squares = squares + jnp.sum((error * error).reshape(BLK // 8, 8, 128), axis=0)
            gn = (2.0 * inv_total) * error / den
            gd = jnp.broadcast_to(-jnp.sum(gn * y, axis=-1, keepdims=True), (BLK, 128))
            gn_s[h, at : at + BLK] = gn
            gd_s[h, at : at + BLK] = gd
            ghi, glo = split(gn.T)
            d = nn(lanes(ghi, glo, ghi), rows(qhi, qhi, qlo))
            dn = jnp.sum(gd * (qhi.astype(F32) + qlo.astype(F32)), axis=0, keepdims=True)
            dblk[h, b] = d
            dblk_norm[h, b] = jnp.broadcast_to(dn, (8, 128))
            d_sum = d_sum + d
            dn_sum = dn_sum + dn
        bwd.own[tile(h)] = d_sum
        bwd.own_norm[line(h)] = dn_sum
        return squares

    def half_outputs(lo, fwd, bwd):
        fwd.finish()
        bwd.own_norm[8:16] = each(lo, lo + half, lambda h, c: outputs(h, c, fwd, bwd), jnp.zeros((8, 128), F32))
        bwd.start()

    half_outputs(0, fwd_a, bwd_a)
    half_outputs(half, fwd_b, bwd_b)

    def loss_cols(dev, src):
        return remote(loss_row, loss_kv.at[src], lk_sems.at[0, dev], lk_sems.at[1, src], dev, "kvh")

    y_ref[...] = tmp[...].astype(BF16)
    save_y.start()

    def local_backward(h, carry, fwd):
        prior = fwd.out[tile(h)]
        prior_norm = fwd.out_norm[line(h)]
        later = jnp.zeros((128, 128), F32)
        later_norm = jnp.zeros((1, 128), F32)
        g = jnp.zeros((128, 128), F32)
        for b in reversed(range(nblk)):
            at = b * BLK
            gn = gn_s[h, at : at + BLK]
            gd = gd_s[h, at : at + BLK]
            vb = vext[at : at + BLK]
            kh = pkh[h, at : at + BLK]
            kl = pkl[h, at : at + BLK]
            qhi = pqh[h, at : at + BLK]
            qlo = pql[h, at : at + BLK]
            ghi, glo = split(gn)
            gf = jnp.where(causal, nt(lanes(ghi, glo), lanes(vb, vb)) + gd, 0.0)
            fhi, flo = split(gf)
            shi, slo = split(prior + loc[h, b])
            norm = prior_norm + loc_norm[h, b, 0:1]
            gqf = nn(lanes(fhi, flo, fhi, ghi, glo, ghi), rows(kh, kh, kl, shi, shi, slo)) + gd * norm
            rhi, rlo = split(back(qhi.astype(F32) + qlo.astype(F32), gqf))
            qtb = qt[h, :, at : at + BLK]
            g = g + nn(lanes(qtb, qtb), rows(rhi, rlo))
            thi, tlo = split(gf.T)
            lhi, llo = split(later)
            gkf[h, at : at + BLK] = (
                nn(lanes(thi, tlo, thi, vb, vb), rows(qhi, qhi, qlo, lhi, llo)) + later_norm
            )
            later = later + dblk[h, b]
            later_norm = later_norm + dblk_norm[h, b, 0:1]
        put(aq, h, g)
        return carry

    def put(ref, h, g):
        g = g.T
        ref[pl.ds(pl.multiple_of(h * 64, 64), 64)] = g[0:64] - g[64:128]

    def backward_a(h, carry):
        return local_backward(h, carry, fwd_a)

    def backward_b(h, carry):
        return local_backward(h, carry, fwd_b)

    each(0, 2, backward_a)
    bwd_a.turn()
    each(2, half, backward_a)
    bwd_b.turn()
    each(half, heads, backward_b)
    q_total = Total(n, me, aq, aq_got, aq_part, aq_out, q_sems)
    k_total = Total(n, me, ak, ak_got, ak_part, ak_out, k_sems)
    q_total.start()

    def key_grads(h, carry, bwd):
        shi, slo = split(bwd.out[tile(h)])
        v = vext[0:tok]
        g = gkf[h] + nn(lanes(v, v), rows(shi, slo)) + bwd.out_norm[line(h)]
        hi, lo = split(back(pkh[h, 0:tok].astype(F32) + pkl[h, 0:tok].astype(F32), g))
        t = kt[...]
        put(ak, h, nn(lanes(t, t), rows(hi, lo)))
        return carry

    bwd_a.finish()
    each(0, half, lambda h, c: key_grads(h, c, bwd_a))
    bwd_b.finish()
    loss_row[...] = bwd_a.out_norm[8:16] + bwd_b.out_norm[8:16]
    peers(m, lambda i: loss_cols(lax.rem(col + i, m), col).start())
    each(half, heads, lambda h, c: key_grads(h, c, bwd_b))
    k_total.start()
    q_total.turn()
    k_total.turn()

    loss_kv[col] = loss_row[...]
    peers(m, lambda i: loss_cols(col, lax.rem(col + i, m)).wait_recv())
    total = lax.fori_loop(0, m, lambda i, t: t + loss_kv[i], jnp.zeros((8, 128), F32))
    loss_ref[0, 0] = jnp.sum(total) * inv_total

    q_total.finish()
    gq_ref[...] = aq_out[...]

    fwd_a.drain()
    fwd_b.drain()
    bwd_a.drain()
    bwd_b.drain()

    @pl.when(me < n - 1)
    def _():
        edge_copy(0, me + 1).wait_send()
        edge_copy(1, me + 1).wait_send()

    peers(m, lambda i: loss_cols(lax.rem(col + i, m), col).wait_send())
    save_y.wait()
    k_total.finish()
    gk_ref[...] = ak_out[...]
    q_total.drain()
    k_total.drain()


def body(queries, keys, values, teacher, q_map, k_map):
    tok, heads, width = queries.shape
    n, m = lax.axis_size("seq"), lax.axis_size("kvh")
    nblk = tok // BLK
    vmem = lambda shape, dtype=F32: pltpu.VMEM(shape, dtype)
    dma = lambda *shape: pltpu.SemaphoreType.DMA(shape)
    state = heads // 2 * 128
    grad = heads * 64
    scan_bufs = lambda: [
        vmem((state, 128)),
        vmem((16, 128)),
        vmem((n, state // n, 128)),
        vmem((n, state // n, 128)),
        vmem((state, 128)),
        vmem((n, 16, 128)),
        vmem((n, 16, 128)),
        vmem((16, 128)),
    ]
    total_bufs = lambda: [vmem((grad, 128)), vmem((n, grad // n, 128)), vmem((grad // n, 128)), vmem((grad, 128))]
    spec = pl.BlockSpec(memory_space=pltpu.VMEM)
    hbm = pl.BlockSpec(memory_space=pl.ANY)
    outs, grad_q, grad_k, loss = pl.pallas_call(
        functools.partial(kernel, n, m, heads, tok, width**-0.5, 1.0 / (tok * n)),
        out_shape=(
            jax.ShapeDtypeStruct((tok * heads, width), BF16),
            jax.ShapeDtypeStruct((grad, width), F32),
            jax.ShapeDtypeStruct((grad, width), F32),
            jax.ShapeDtypeStruct((1, 1), F32),
        ),
        in_specs=[hbm, spec, spec, hbm, spec, spec],
        out_specs=(hbm, spec, spec, pl.BlockSpec(memory_space=pltpu.SMEM)),
        scratch_shapes=[
            vmem((tok * heads, width)),
            vmem((tok + 2 * WIN, 128), BF16),
            vmem((tok + 2 * WIN, 128), BF16),
            vmem((tok + 2 * WIN, 256), BF16),
            vmem((256, tok), BF16),
            vmem((128, tok), BF16),
            vmem((heads, tok, 128), BF16),
            vmem((heads, 128, tok), BF16),
            vmem((heads, tok, 128), BF16),
            vmem((heads, tok, 128), BF16),
            vmem((heads, tok + WIN, 128), BF16),
            vmem((heads, tok + WIN, 128), BF16),
            scan_bufs(),
            scan_bufs(),
            vmem((heads, nblk, 128, 128)),
            vmem((heads, nblk, 8, 128)),
            vmem((heads, tok, 256)),
            vmem((heads, tok, 128)),
            vmem((heads, tok, 128)),
            vmem((heads, nblk, 128, 128)),
            vmem((heads, nblk, 8, 128)),
            scan_bufs(),
            scan_bufs(),
            vmem((heads, tok, 128)),
            *total_bufs(),
            *total_bufs(),
            vmem((8, 128)),
            vmem((m, 8, 128)),
            vmem((tok * heads, width), BF16),
            vmem((tok * heads, width), BF16),
            vmem((tok * heads, width), BF16),
            (dma(4), dma(4)),
            (dma(4), dma(4)),
            (dma(4), dma(4)),
            (dma(4), dma(4)),
            dma(4),
            dma(4),
            dma(2, 2),
            dma(2, m),
            dma(3),
        ],
        compiler_params=pltpu.CompilerParams(collective_id=1, has_side_effects=True, vmem_limit_bytes=58 << 20),
    )(
        queries.reshape(tok * heads, width),
        keys.reshape(tok, width),
        values.reshape(tok, width),
        teacher.reshape(tok * heads, width),
        jnp.swapaxes(q_map, 1, 2),
        jnp.swapaxes(k_map, 1, 2),
    )
    unmap = lambda g: jnp.swapaxes(g.reshape(heads, 64, width), 1, 2)
    return outs.reshape(tok, heads, width), unmap(grad_q), unmap(grad_k), loss.reshape(())


def solution(mesh):
    in_specs = (
        P("seq", "kvh", None),
        P("seq", "kvh", None),
        P("seq", "kvh", None),
        P("seq", "kvh", None),
        P("kvh", None, None),
        P("kvh", None, None),
    )
    out_specs = (P("seq", "kvh", None), P("kvh", None, None), P("kvh", None, None), P())
    return jax.shard_map(body, mesh=mesh, in_specs=in_specs, out_specs=out_specs, check_vma=False)
```

```python
import functools

import jax
import jax.numpy as jnp
from jax import lax
from jax.experimental import pallas as pl
from jax.experimental.pallas import tpu as pltpu
from jax.sharding import PartitionSpec as P

WIN = 64
BLK = 128
F32, BF16 = jnp.float32, jnp.bfloat16
MESH = pl.DeviceIdType.MESH


def split(x):
    hi = x.astype(BF16)
    return hi, (x - hi.astype(F32)).astype(BF16)


def nn(a, b):
    return lax.dot_general(a, b, (((1,), (0,)), ((), ())), preferred_element_type=F32)


def nt(a, b):
    return lax.dot_general(a, b, (((1,), (1,)), ((), ())), preferred_element_type=F32)


def lanes(*parts):
    return jnp.concatenate(parts, axis=1)


def rows(*parts):
    return jnp.concatenate(parts, axis=0)


def peers(n, fn):
    def go(i, carry):
        fn(i)
        return carry

    lax.fori_loop(1, n, go, 0)


def remote(src, dst, send, recv, dev, axis="seq"):
    return pltpu.make_async_remote_copy(
        src_ref=src, dst_ref=dst, send_sem=send, recv_sem=recv, device_id={axis: dev}, device_id_type=MESH
    )


class Scan:
    def __init__(self, n, me, own, own_norm, got, part, out, got_norm, part_norm, out_norm, sems, norm_sems, reverse, keeper):
        self.__dict__.update(locals())
        self.chunk = own.shape[0] // n

    def piece(self, dev):
        return pl.ds(pl.multiple_of(dev * self.chunk, 8), self.chunk)

    def next(self):
        return lax.rem(self.me + 1, self.n)

    def first(self, dev):
        return remote(self.own.at[self.piece(dev)], self.got.at[self.me], self.sems.at[0], self.sems.at[1], dev)

    def second(self, dev):
        return remote(self.part.at[dev], self.out.at[self.piece(self.me)], self.sems.at[2], self.sems.at[3], dev)

    def all_first(self):
        block = self.got.at[pl.ds(0, self.n - 1)]
        return remote(block, block, self.sems.at[0], self.sems.at[1], self.next())

    def all_second(self):
        block = self.out.at[pl.ds(0, (self.n - 1) * self.chunk)]
        return remote(block, block, self.sems.at[2], self.sems.at[3], self.next())

    def norm_first(self):
        return remote(self.own_norm, self.got_norm.at[self.me], self.norm_sems.at[0], self.norm_sems.at[1], self.keeper)

    def norm_second(self, dev):
        return remote(self.part_norm.at[dev], self.out_norm, self.norm_sems.at[2], self.norm_sems.at[3], dev)

    def all_norms(self):
        block = self.got_norm.at[pl.ds(0, self.n - 1)]
        return remote(block, block, self.norm_sems.at[2], self.norm_sems.at[1], self.next())

    def start(self):
        n, me = self.n, self.me
        peers(n, lambda i: self.first(lax.rem(me + i, n)).start())

        @pl.when(me != self.keeper)
        def _():
            self.norm_first().start()

    def sums(self, got, part, zero):
        n = self.n

        def go(i, total):
            at = n - 1 - i if self.reverse else i
            part[at] = total
            return total + got[at]

        return lax.fori_loop(0, n, go, zero)

    def turn(self):
        n, me, keeper = self.n, self.me, self.keeper
        self.got[me] = self.own[self.piece(me)]
        self.all_first().wait_recv()
        self.sums(self.got, self.part, jnp.zeros((self.chunk, 128), F32))
        peers(n, lambda i: self.second(lax.rem(me + i, n)).start())
        self.out[self.piece(me)] = self.part[me]

        @pl.when(me == keeper)
        def _():
            self.got_norm[keeper] = self.own_norm[...]
            self.all_norms().wait_recv()
            total = self.sums(self.got_norm, self.part_norm, jnp.zeros((16, 128), F32))
            self.part_norm[:, 8:16] = jnp.broadcast_to(total[None, 8:16], (n, 8, 128))
            peers(n, lambda i: self.norm_second(lax.rem(keeper + i, n)).start())
            self.out_norm[...] = self.part_norm[keeper]

    def finish(self):
        self.all_second().wait_recv()

        @pl.when(self.me != self.keeper)
        def _():
            self.norm_second(self.next()).wait_recv()

    def drain(self):
        self.all_first().wait_send()
        self.all_second().wait_send()

        @pl.when(self.me != self.keeper)
        def _():
            self.norm_first().wait_send()

        @pl.when(self.me == self.keeper)
        def _():
            self.all_norms().wait_send()


class Total:
    def __init__(self, n, me, own, got, part, out, sems):
        self.__dict__.update(locals())
        self.chunk = own.shape[0] // n

    def piece(self, dev):
        return pl.ds(pl.multiple_of(dev * self.chunk, 8), self.chunk)

    def next(self):
        return lax.rem(self.me + 1, self.n)

    def first(self, dev):
        return remote(self.own.at[self.piece(dev)], self.got.at[self.me], self.sems.at[0], self.sems.at[1], dev)

    def second(self, dev):
        return remote(self.part, self.out.at[self.piece(self.me)], self.sems.at[2], self.sems.at[3], dev)

    def all_first(self):
        block = self.got.at[pl.ds(0, self.n - 1)]
        return remote(block, block, self.sems.at[0], self.sems.at[1], self.next())

    def all_second(self):
        block = self.out.at[pl.ds(0, (self.n - 1) * self.chunk)]
        return remote(block, block, self.sems.at[2], self.sems.at[3], self.next())

    def start(self):
        peers(self.n, lambda i: self.first(lax.rem(self.me + i, self.n)).start())

    def turn(self):
        n, me = self.n, self.me
        self.got[me] = self.own[self.piece(me)]
        self.all_first().wait_recv()
        self.part[...] = lax.fori_loop(0, n, lambda i, t: t + self.got[i], jnp.zeros((self.chunk, 128), F32))
        peers(n, lambda i: self.second(lax.rem(me + i, n)).start())
        self.out[self.piece(me)] = self.part[...]

    def finish(self):
        self.all_second().wait_recv()

    def drain(self):
        self.all_first().wait_send()
        self.all_second().wait_send()


def each(lo, hi, fn, init=0, unroll=2):
    def go(i, carry):
        for u in range(unroll):
            carry = fn(lo + i * unroll + u, carry)
        return carry

    return lax.fori_loop(0, (hi - lo) // unroll, go, init)


def kernel(n, m, heads, tok, scale, inv_total, q_hbm, k_ref, v_ref, t_hbm, wq_ref, wk_ref,
           y_hbm, gq_ref, gk_ref, loss_ref,
           tmp, kext, vext, vaug, vaugt, kt, qh, qt, pqh, pql, pkh, pkl,
           bufs_fa, bufs_fb,
           loc, loc_norm, numer, gn_s, gd_s, dblk, dblk_norm,
           bufs_ba, bufs_bb,
           gkf, bufs_qa, bufs_qb, bufs_ka, bufs_kb,
           loss_row, loss_kv, q_ref, t_ref, y_ref,
           sems_fa, sems_fb, sems_ba, sems_bb, sems_qa, sems_qb, sems_ka, sems_kb, e_sems, lk_sems, io_sems):
    me = lax.axis_index("seq")
    col = lax.axis_index("kvh")
    nblk = tok // BLK
    half = heads // 2

    barrier = pltpu.get_barrier_semaphore()
    peers(n, lambda i: pl.semaphore_signal(barrier, inc=1, device_id={"seq": lax.rem(me + i, n)}, device_id_type=MESH))
    peers(m, lambda i: pl.semaphore_signal(barrier, inc=1, device_id={"kvh": lax.rem(col + i, m)}, device_id_type=MESH))
    load_q = pltpu.make_async_copy(q_hbm, q_ref, io_sems.at[0])
    load_t = pltpu.make_async_copy(t_hbm, t_ref, io_sems.at[1])
    save_y = pltpu.make_async_copy(y_ref, y_hbm, io_sems.at[2])
    load_q.start()
    load_t.start()

    lane = lax.broadcasted_iota(jnp.int32, (1, 128), 1)
    upper = lane < 64
    ri = lax.broadcasted_iota(jnp.int32, (256, 128), 0)
    ci = lax.broadcasted_iota(jnp.int32, (256, 128), 1)
    ones2 = jnp.where((lax.rem(ri, 128) < 64) == (ci < 64), 1.0, 0.0).astype(BF16)

    def half_sums(x):
        hi, lo = split(x)
        return nn(lanes(hi, lo), ones2)

    def maps(x, w):
        w = w.astype(F32)
        a = nt(x, rows(w, -w).astype(BF16))
        low = jnp.full_like(a, -jnp.inf)
        top = jnp.where(
            upper,
            jnp.max(jnp.where(upper, a, low), axis=-1, keepdims=True),
            jnp.max(jnp.where(upper, low, a), axis=-1, keepdims=True),
        )
        e = jnp.exp(a - top)
        return e / half_sums(e)

    def back(phi, g):
        return phi * (g - half_sums(phi * g))

    fwd_a = Scan(n, me, *bufs_fa, *sems_fa, False, n // 2)
    fwd_b = Scan(n, me, *bufs_fb, *sems_fb, False, n // 2 - 1)
    bwd_a = Scan(n, me, *bufs_ba, *sems_ba, True, n // 2)
    bwd_b = Scan(n, me, *bufs_bb, *sems_bb, True, n // 2 - 1)

    def tile(h):
        return pl.ds(pl.multiple_of(lax.rem(h, half) * 128, 128), 128)

    def line(h):
        return pl.ds(lax.rem(h, half), 1)

    kext[WIN : WIN + tok] = k_ref[...]
    vext[WIN : WIN + tok] = v_ref[...]
    vt = v_ref[...].astype(F32).T.astype(BF16)
    vt2 = lanes(vt, vt)

    def own_keys(scan):
        def own_keys(h, carry):
            phi = maps(k_ref[...], wk_ref[h])
            hi, lo = split(phi)
            pkh[h, WIN : WIN + tok] = hi
            pkl[h, WIN : WIN + tok] = lo
            scan.own[tile(h)] = nn(vt2, rows(hi, lo))
            scan.own_norm[line(h)] = jnp.sum(phi, axis=0, keepdims=True)
            return carry

        return own_keys

    fwd_a.own_norm[...] = jnp.zeros((16, 128), F32)
    fwd_b.own_norm[...] = jnp.zeros((16, 128), F32)
    bwd_a.own_norm[...] = jnp.zeros((16, 128), F32)
    bwd_b.own_norm[...] = jnp.zeros((16, 128), F32)
    each(0, half, own_keys(fwd_a))
    each(half, heads, own_keys(fwd_b))

    load_q.wait()
    tmp[...] = q_ref[...].astype(F32)

    def query_maps(h, carry):
        f = tmp[pl.ds(h, tok, stride=heads), :]
        x = f.astype(BF16)
        qh[h] = x
        qt[h] = f.T.astype(BF16)
        hi, lo = split(maps(x, wq_ref[h]))
        pqh[h] = hi
        pql[h] = lo
        return carry

    each(0, heads, query_maps)
    pl.semaphore_wait(barrier, n - 1 + m - 1)

    def edge_copy(i, dev):
        src, dst = (k_ref, kext) if i == 0 else (v_ref, vext)
        return remote(src.at[pl.ds(tok - WIN, WIN)], dst.at[pl.ds(0, WIN)], e_sems.at[0, i], e_sems.at[1, i], dev)

    @pl.when(me < n - 1)
    def _():
        edge_copy(0, me + 1).start()
        edge_copy(1, me + 1).start()


    fwd_a.start()
    fwd_b.start()

    @pl.when(me == 0)
    def _():
        kext[0:WIN] = jnp.zeros((WIN, 128), BF16)
        vext[0:WIN] = jnp.zeros((WIN, 128), BF16)

    @pl.when(me > 0)
    def _():
        edge_copy(0, me - 1).wait_recv()
        edge_copy(1, me - 1).wait_recv()

    pad = jnp.zeros((WIN, 128), BF16)
    kext[WIN + tok :] = pad
    vext[WIN + tok :] = pad
    valid = jnp.where(me > 0, 1.0, 0.0).astype(F32)
    vaug[:, 0:128] = vext[...]
    vaug[:, 128:256] = jnp.ones((tok + 2 * WIN, 128), BF16)
    vaugt[0:128] = vext[0:tok].astype(F32).T.astype(BF16)
    vaugt[128:256] = jnp.ones((128, tok), BF16)
    kt[...] = kext[0:tok].astype(F32).T.astype(BF16)

    def edge_maps(h, carry):
        phi = maps(kext[0:WIN], wk_ref[h]) * valid
        hi, lo = split(phi)
        pkh[h, 0:WIN] = hi
        pkl[h, 0:WIN] = lo
        return carry

    each(0, heads, edge_maps)

    r2 = lax.broadcasted_iota(jnp.int32, (BLK, 2 * BLK), 0)
    c2 = lax.broadcasted_iota(jnp.int32, (BLK, 2 * BLK), 1)
    near_band = (c2 > r2) & (c2 <= r2 + WIN)
    first_key = jnp.where(me > 0, 0, WIN)
    r1 = lax.broadcasted_iota(jnp.int32, (BLK, BLK), 0)
    c1 = lax.broadcasted_iota(jnp.int32, (BLK, BLK), 1)
    causal = c1 <= r1

    def local_forward(h, carry):
        ph0 = pkh[h, 0:WIN]
        pl0 = pkl[h, 0:WIN]
        zero = jnp.zeros((WIN, 128), BF16)
        vb = vaugt[:, 0:BLK]
        state = -nn(lanes(vb, vb), rows(ph0, zero, pl0, zero))
        for b in range(nblk):
            at = b * BLK
            loc[h, b] = state[0:128]
            loc_norm[h, b] = state[128:136]
            kh = pkh[h, at : at + BLK]
            kl = pkl[h, at : at + BLK]
            qhi = pqh[h, at : at + BLK]
            qlo = pql[h, at : at + BLK]
            q3 = lanes(qhi, qlo, qhi)
            far = jnp.where(causal, nt(q3, lanes(kh, kh, kl)), 0.0)
            s = nt(qh[h, at : at + BLK], kext[at : at + 2 * BLK]) * scale
            mask = near_band & (c2 >= first_key) if b == 0 else near_band
            s = jnp.where(mask, s, -1e30)
            top = jnp.max(s, axis=-1, keepdims=True)
            w = jnp.where(mask, jnp.exp(s - top), 0.0)
            w = lanes(w[:, 0:BLK] + far, w[:, BLK:])
            whi, wlo = split(w)
            va = vaug[at : at + 2 * BLK]
            shi, slo = split(state)
            numer[h, at : at + BLK] = nn(lanes(whi, wlo), rows(va, va)) + nt(q3, lanes(shi, shi, slo))
            if b + 1 < nblk:
                vb = vaugt[:, at : at + BLK]
                state = state + nn(lanes(vb, vb), rows(kh, kl))
        return carry

    each(0, half, local_forward)
    fwd_a.turn()
    each(half, half + 2, local_forward)
    fwd_b.turn()
    each(half + 2, heads, local_forward)

    load_t.wait()
    tmp[...] = t_ref[...].astype(F32)

    def outputs(h, squares, fwd, bwd):
        prior = fwd.out[tile(h)]
        prior_norm = jnp.broadcast_to(fwd.out_norm[line(h)], (128, 128))
        shi, slo = split(rows(prior, prior_norm))
        s3 = lanes(shi, shi, slo)
        d_sum = jnp.zeros((128, 128), F32)
        dn_sum = jnp.zeros((1, 128), F32)
        for b in range(nblk):
            at = b * BLK
            qhi = pqh[h, at : at + BLK]
            qlo = pql[h, at : at + BLK]
            both = numer[h, at : at + BLK] + nt(lanes(qhi, qlo, qhi), s3)
            den = both[:, 128:256]
            y = both[:, 0:128] / den
            where = pl.ds(h + at * heads, BLK, stride=heads)
            error = y - tmp[where, :]
            tmp[where, :] = y
            squares = squares + jnp.sum((error * error).reshape(BLK // 8, 8, 128), axis=0)
            gn = (2.0 * inv_total) * error / den
            gd = jnp.broadcast_to(-jnp.sum(gn * y, axis=-1, keepdims=True), (BLK, 128))
            gn_s[h, at : at + BLK] = gn
            gd_s[h, at : at + BLK] = gd
            ghi, glo = split(gn.T)
            d = nn(lanes(ghi, glo, ghi), rows(qhi, qhi, qlo))
            dn = jnp.sum(gd * (qhi.astype(F32) + qlo.astype(F32)), axis=0, keepdims=True)
            dblk[h, b] = d
            dblk_norm[h, b] = jnp.broadcast_to(dn, (8, 128))
            d_sum = d_sum + d
            dn_sum = dn_sum + dn
        bwd.own[tile(h)] = d_sum
        bwd.own_norm[line(h)] = dn_sum
        return squares

    def half_outputs(lo, fwd, bwd):
        fwd.finish()
        bwd.own_norm[8:16] = each(lo, lo + half, lambda h, c: outputs(h, c, fwd, bwd), jnp.zeros((8, 128), F32))
        bwd.start()

    half_outputs(0, fwd_a, bwd_a)
    half_outputs(half, fwd_b, bwd_b)

    def loss_cols(dev, src):
        return remote(loss_row, loss_kv.at[src], lk_sems.at[0, dev], lk_sems.at[1, src], dev, "kvh")

    y_ref[...] = tmp[...].astype(BF16)
    save_y.start()

    def local_backward(h, carry, fwd, into):
        prior = fwd.out[tile(h)]
        prior_norm = fwd.out_norm[line(h)]
        later = jnp.zeros((128, 128), F32)
        later_norm = jnp.zeros((1, 128), F32)
        g = jnp.zeros((128, 128), F32)
        for b in reversed(range(nblk)):
            at = b * BLK
            gn = gn_s[h, at : at + BLK]
            gd = gd_s[h, at : at + BLK]
            vb = vext[at : at + BLK]
            kh = pkh[h, at : at + BLK]
            kl = pkl[h, at : at + BLK]
            qhi = pqh[h, at : at + BLK]
            qlo = pql[h, at : at + BLK]
            ghi, glo = split(gn)
            gf = jnp.where(causal, nt(lanes(ghi, glo), lanes(vb, vb)) + gd, 0.0)
            fhi, flo = split(gf)
            shi, slo = split(prior + loc[h, b])
            norm = prior_norm + loc_norm[h, b, 0:1]
            gqf = nn(lanes(fhi, flo, fhi, ghi, glo, ghi), rows(kh, kh, kl, shi, shi, slo)) + gd * norm
            rhi, rlo = split(back(qhi.astype(F32) + qlo.astype(F32), gqf))
            qtb = qt[h, :, at : at + BLK]
            g = g + nn(lanes(qtb, qtb), rows(rhi, rlo))
            thi, tlo = split(gf.T)
            lhi, llo = split(later)
            gkf[h, at : at + BLK] = (
                nn(lanes(thi, tlo, thi, vb, vb), rows(qhi, qhi, qlo, lhi, llo)) + later_norm
            )
            later = later + dblk[h, b]
            later_norm = later_norm + dblk_norm[h, b, 0:1]
        put(into, h, g)
        return carry

    def put(ref, h, g):
        g = g.T
        ref[pl.ds(pl.multiple_of(lax.rem(h, half) * 64, 64), 64)] = g[0:64] - g[64:128]

    q_a = Total(n, me, *bufs_qa, sems_qa)
    q_b = Total(n, me, *bufs_qb, sems_qb)
    k_a = Total(n, me, *bufs_ka, sems_ka)
    k_b = Total(n, me, *bufs_kb, sems_kb)

    def backward_a(h, carry):
        return local_backward(h, carry, fwd_a, q_a.own)

    def backward_b(h, carry):
        return local_backward(h, carry, fwd_b, q_b.own)

    each(0, 2, backward_a)
    bwd_a.turn()
    each(2, half, backward_a)
    bwd_b.turn()
    q_a.start()
    each(half, heads, backward_b)
    q_b.start()
    q_a.turn()

    def key_grads(h, carry, bwd, into):
        shi, slo = split(bwd.out[tile(h)])
        v = vext[0:tok]
        g = gkf[h] + nn(lanes(v, v), rows(shi, slo)) + bwd.out_norm[line(h)]
        hi, lo = split(back(pkh[h, 0:tok].astype(F32) + pkl[h, 0:tok].astype(F32), g))
        t = kt[...]
        put(into, h, nn(lanes(t, t), rows(hi, lo)))
        return carry

    bwd_a.finish()
    each(0, half, lambda h, c: key_grads(h, c, bwd_a, k_a.own))
    k_a.start()
    bwd_b.finish()
    loss_row[...] = bwd_a.out_norm[8:16] + bwd_b.out_norm[8:16]
    peers(m, lambda i: loss_cols(lax.rem(col + i, m), col).start())
    each(half, heads, lambda h, c: key_grads(h, c, bwd_b, k_b.own))
    k_b.start()
    q_b.turn()
    k_a.turn()
    k_b.turn()

    loss_kv[col] = loss_row[...]
    peers(m, lambda i: loss_cols(col, lax.rem(col + i, m)).wait_recv())
    total = lax.fori_loop(0, m, lambda i, t: t + loss_kv[i], jnp.zeros((8, 128), F32))
    loss_ref[0, 0] = jnp.sum(total) * inv_total

    cut = half * 64
    q_a.finish()
    gq_ref[0:cut] = q_a.out[...]
    q_b.finish()
    gq_ref[cut:] = q_b.out[...]

    fwd_a.drain()
    fwd_b.drain()
    bwd_a.drain()
    bwd_b.drain()

    @pl.when(me < n - 1)
    def _():
        edge_copy(0, me + 1).wait_send()
        edge_copy(1, me + 1).wait_send()

    peers(m, lambda i: loss_cols(lax.rem(col + i, m), col).wait_send())
    save_y.wait()
    q_a.drain()
    q_b.drain()
    k_a.finish()
    gk_ref[0:cut] = k_a.out[...]
    k_b.finish()
    gk_ref[cut:] = k_b.out[...]
    k_a.drain()
    k_b.drain()


def body(queries, keys, values, teacher, q_map, k_map):
    tok, heads, width = queries.shape
    n, m = lax.axis_size("seq"), lax.axis_size("kvh")
    nblk = tok // BLK
    vmem = lambda shape, dtype=F32: pltpu.VMEM(shape, dtype)
    dma = lambda *shape: pltpu.SemaphoreType.DMA(shape)
    state = heads // 2 * 128
    grad = heads * 64
    scan_bufs = lambda: [
        vmem((state, 128)),
        vmem((16, 128)),
        vmem((n, state // n, 128)),
        vmem((n, state // n, 128)),
        vmem((state, 128)),
        vmem((n, 16, 128)),
        vmem((n, 16, 128)),
        vmem((16, 128)),
    ]
    part = grad // 2
    total_bufs = lambda: [vmem((part, 128)), vmem((n, part // n, 128)), vmem((part // n, 128)), vmem((part, 128))]
    spec = pl.BlockSpec(memory_space=pltpu.VMEM)
    hbm = pl.BlockSpec(memory_space=pl.ANY)
    outs, grad_q, grad_k, loss = pl.pallas_call(
        functools.partial(kernel, n, m, heads, tok, width**-0.5, 1.0 / (tok * n)),
        out_shape=(
            jax.ShapeDtypeStruct((tok * heads, width), BF16),
            jax.ShapeDtypeStruct((grad, width), F32),
            jax.ShapeDtypeStruct((grad, width), F32),
            jax.ShapeDtypeStruct((1, 1), F32),
        ),
        in_specs=[hbm, spec, spec, hbm, spec, spec],
        out_specs=(hbm, spec, spec, pl.BlockSpec(memory_space=pltpu.SMEM)),
        scratch_shapes=[
            vmem((tok * heads, width)),
            vmem((tok + 2 * WIN, 128), BF16),
            vmem((tok + 2 * WIN, 128), BF16),
            vmem((tok + 2 * WIN, 256), BF16),
            vmem((256, tok), BF16),
            vmem((128, tok), BF16),
            vmem((heads, tok, 128), BF16),
            vmem((heads, 128, tok), BF16),
            vmem((heads, tok, 128), BF16),
            vmem((heads, tok, 128), BF16),
            vmem((heads, tok + WIN, 128), BF16),
            vmem((heads, tok + WIN, 128), BF16),
            scan_bufs(),
            scan_bufs(),
            vmem((heads, nblk, 128, 128)),
            vmem((heads, nblk, 8, 128)),
            vmem((heads, tok, 256)),
            vmem((heads, tok, 128)),
            vmem((heads, tok, 128)),
            vmem((heads, nblk, 128, 128)),
            vmem((heads, nblk, 8, 128)),
            scan_bufs(),
            scan_bufs(),
            vmem((heads, tok, 128)),
            total_bufs(),
            total_bufs(),
            total_bufs(),
            total_bufs(),
            vmem((8, 128)),
            vmem((m, 8, 128)),
            vmem((tok * heads, width), BF16),
            vmem((tok * heads, width), BF16),
            vmem((tok * heads, width), BF16),
            (dma(4), dma(4)),
            (dma(4), dma(4)),
            (dma(4), dma(4)),
            (dma(4), dma(4)),
            dma(4),
            dma(4),
            dma(4),
            dma(4),
            dma(2, 2),
            dma(2, m),
            dma(3),
        ],
        compiler_params=pltpu.CompilerParams(collective_id=1, has_side_effects=True, vmem_limit_bytes=58 << 20),
    )(
        queries.reshape(tok * heads, width),
        keys.reshape(tok, width),
        values.reshape(tok, width),
        teacher.reshape(tok * heads, width),
        jnp.swapaxes(q_map, 1, 2),
        jnp.swapaxes(k_map, 1, 2),
    )
    unmap = lambda g: jnp.swapaxes(g.reshape(heads, 64, width), 1, 2)
    return outs.reshape(tok, heads, width), unmap(grad_q), unmap(grad_k), loss.reshape(())


def solution(mesh):
    in_specs = (
        P("seq", "kvh", None),
        P("seq", "kvh", None),
        P("seq", "kvh", None),
        P("seq", "kvh", None),
        P("kvh", None, None),
        P("kvh", None, None),
    )
    out_specs = (P("seq", "kvh", None), P("kvh", None, None), P("kvh", None, None), P())
    return jax.shard_map(body, mesh=mesh, in_specs=in_specs, out_specs=out_specs, check_vma=False)
```

```python
import functools

import jax
import jax.numpy as jnp
from jax import lax
from jax.experimental import pallas as pl
from jax.experimental.pallas import tpu as pltpu
from jax.sharding import PartitionSpec as P

WIN = 64
BLK = 128
F32, BF16 = jnp.float32, jnp.bfloat16
MESH = pl.DeviceIdType.MESH


def split(x):
    hi = x.astype(BF16)
    return hi, (x - hi.astype(F32)).astype(BF16)


def nn(a, b):
    return lax.dot_general(a, b, (((1,), (0,)), ((), ())), preferred_element_type=F32)


def nt(a, b):
    return lax.dot_general(a, b, (((1,), (1,)), ((), ())), preferred_element_type=F32)


def lanes(*parts):
    return jnp.concatenate(parts, axis=1)


def rows(*parts):
    return jnp.concatenate(parts, axis=0)


def peers(n, fn):
    def go(i, carry):
        fn(i)
        return carry

    lax.fori_loop(1, n, go, 0)


def remote(src, dst, send, recv, dev, axis="seq"):
    return pltpu.make_async_remote_copy(
        src_ref=src, dst_ref=dst, send_sem=send, recv_sem=recv, device_id={axis: dev}, device_id_type=MESH
    )


class Scan:
    def __init__(self, n, me, own, own_norm, got, part, out, got_norm, part_norm, out_norm, sems, norm_sems, reverse, keeper):
        self.__dict__.update(locals())
        self.chunk = own.shape[0] // n

    def piece(self, dev):
        return pl.ds(pl.multiple_of(dev * self.chunk, 8), self.chunk)

    def next(self):
        return lax.rem(self.me + 1, self.n)

    def first(self, dev):
        return remote(self.own.at[self.piece(dev)], self.got.at[self.me], self.sems.at[0], self.sems.at[1], dev)

    def second(self, dev):
        return remote(self.part.at[dev], self.out.at[self.piece(self.me)], self.sems.at[2], self.sems.at[3], dev)

    def all_first(self):
        block = self.got.at[pl.ds(0, self.n - 1)]
        return remote(block, block, self.sems.at[0], self.sems.at[1], self.next())

    def all_second(self):
        block = self.out.at[pl.ds(0, (self.n - 1) * self.chunk)]
        return remote(block, block, self.sems.at[2], self.sems.at[3], self.next())

    def norm_first(self):
        return remote(self.own_norm, self.got_norm.at[self.me], self.norm_sems.at[0], self.norm_sems.at[1], self.keeper)

    def norm_second(self, dev):
        return remote(self.part_norm.at[dev], self.out_norm, self.norm_sems.at[2], self.norm_sems.at[3], dev)

    def all_norms(self):
        block = self.got_norm.at[pl.ds(0, self.n - 1)]
        return remote(block, block, self.norm_sems.at[2], self.norm_sems.at[1], self.next())

    def start(self):
        n, me = self.n, self.me
        peers(n, lambda i: self.first(lax.rem(me + i, n)).start())

        @pl.when(me != self.keeper)
        def _():
            self.norm_first().start()

    def sums(self, got, part, zero):
        n = self.n

        def go(i, total):
            at = n - 1 - i if self.reverse else i
            part[at] = total
            return total + got[at]

        return lax.fori_loop(0, n, go, zero)

    def turn(self):
        n, me, keeper = self.n, self.me, self.keeper
        self.got[me] = self.own[self.piece(me)]
        self.all_first().wait_recv()
        self.sums(self.got, self.part, jnp.zeros((self.chunk, 128), F32))
        peers(n, lambda i: self.second(lax.rem(me + i, n)).start())
        self.out[self.piece(me)] = self.part[me]

        @pl.when(me == keeper)
        def _():
            self.got_norm[keeper] = self.own_norm[...]
            self.all_norms().wait_recv()
            total = self.sums(self.got_norm, self.part_norm, jnp.zeros((16, 128), F32))
            self.part_norm[:, 8:16] = jnp.broadcast_to(total[None, 8:16], (n, 8, 128))
            peers(n, lambda i: self.norm_second(lax.rem(keeper + i, n)).start())
            self.out_norm[...] = self.part_norm[keeper]

    def finish(self):
        self.all_second().wait_recv()

        @pl.when(self.me != self.keeper)
        def _():
            self.norm_second(self.next()).wait_recv()

    def drain(self):
        self.all_first().wait_send()
        self.all_second().wait_send()

        @pl.when(self.me != self.keeper)
        def _():
            self.norm_first().wait_send()

        @pl.when(self.me == self.keeper)
        def _():
            self.all_norms().wait_send()


class Total:
    def __init__(self, n, me, own, got, part, out, sems):
        self.__dict__.update(locals())
        self.chunk = own.shape[0] // n

    def piece(self, dev):
        return pl.ds(pl.multiple_of(dev * self.chunk, 8), self.chunk)

    def next(self):
        return lax.rem(self.me + 1, self.n)

    def first(self, dev):
        return remote(self.own.at[self.piece(dev)], self.got.at[self.me], self.sems.at[0], self.sems.at[1], dev)

    def second(self, dev):
        return remote(self.part, self.out.at[self.piece(self.me)], self.sems.at[2], self.sems.at[3], dev)

    def all_first(self):
        block = self.got.at[pl.ds(0, self.n - 1)]
        return remote(block, block, self.sems.at[0], self.sems.at[1], self.next())

    def all_second(self):
        block = self.out.at[pl.ds(0, (self.n - 1) * self.chunk)]
        return remote(block, block, self.sems.at[2], self.sems.at[3], self.next())

    def start(self):
        peers(self.n, lambda i: self.first(lax.rem(self.me + i, self.n)).start())

    def turn(self):
        n, me = self.n, self.me
        self.got[me] = self.own[self.piece(me)]
        self.all_first().wait_recv()
        self.part[...] = lax.fori_loop(0, n, lambda i, t: t + self.got[i], jnp.zeros((self.chunk, 128), F32))
        peers(n, lambda i: self.second(lax.rem(me + i, n)).start())
        self.out[self.piece(me)] = self.part[...]

    def finish(self):
        self.all_second().wait_recv()

    def drain(self):
        self.all_first().wait_send()
        self.all_second().wait_send()


def each(lo, hi, fn, init=0, unroll=2):
    def go(i, carry):
        for u in range(unroll):
            carry = fn(lo + i * unroll + u, carry)
        return carry

    return lax.fori_loop(0, (hi - lo) // unroll, go, init)


def kernel(n, m, heads, tok, scale, inv_total, q_hbm, k_ref, v_ref, t_hbm, wq_ref, wk_ref,
           y_hbm, gq_ref, gk_ref, loss_ref,
           tmp, kext, vext, vaug, vaugt, kt, qh, qt, pqh, pql, pkh, pkl,
           bufs_fa, bufs_fb,
           loc, loc_norm, numer, gn_s, gd_s, dblk, dblk_norm,
           bufs_ba, bufs_bb,
           gkf, aq, aq_got, aq_part, aq_out, ak, ak_got, ak_part, ak_out,
           loss_row, loss_kv, q_ref, t_ref, y_ref,
           sems_fa, sems_fb, sems_ba, sems_bb, q_sems, k_sems, e_sems, lk_sems, io_sems):
    me = lax.axis_index("seq")
    col = lax.axis_index("kvh")
    nblk = tok // BLK
    half = heads // 2

    barrier = pltpu.get_barrier_semaphore()
    peers(n, lambda i: pl.semaphore_signal(barrier, inc=1, device_id={"seq": lax.rem(me + i, n)}, device_id_type=MESH))
    peers(m, lambda i: pl.semaphore_signal(barrier, inc=1, device_id={"kvh": lax.rem(col + i, m)}, device_id_type=MESH))
    load_q = pltpu.make_async_copy(q_hbm, q_ref, io_sems.at[0])
    load_t = pltpu.make_async_copy(t_hbm, t_ref, io_sems.at[1])
    save_y = pltpu.make_async_copy(y_ref, y_hbm, io_sems.at[2])
    load_q.start()
    load_t.start()

    lane = lax.broadcasted_iota(jnp.int32, (1, 128), 1)
    upper = lane < 64
    ri = lax.broadcasted_iota(jnp.int32, (256, 128), 0)
    ci = lax.broadcasted_iota(jnp.int32, (256, 128), 1)
    ones2 = jnp.where((lax.rem(ri, 128) < 64) == (ci < 64), 1.0, 0.0).astype(BF16)

    def half_sums(x):
        hi, lo = split(x)
        return nn(lanes(hi, lo), ones2)

    def maps(x, w):
        w = w.astype(F32)
        a = nt(x, rows(w, -w).astype(BF16))
        low = jnp.full_like(a, -jnp.inf)
        top = jnp.where(
            upper,
            jnp.max(jnp.where(upper, a, low), axis=-1, keepdims=True),
            jnp.max(jnp.where(upper, low, a), axis=-1, keepdims=True),
        )
        e = jnp.exp(a - top)
        return e / half_sums(e)

    def back(phi, g):
        return phi * (g - half_sums(phi * g))

    fwd_a = Scan(n, me, *bufs_fa, *sems_fa, False, n // 2)
    fwd_b = Scan(n, me, *bufs_fb, *sems_fb, False, n // 2 - 1)
    bwd_a = Scan(n, me, *bufs_ba, *sems_ba, True, n // 2)
    bwd_b = Scan(n, me, *bufs_bb, *sems_bb, True, n // 2 - 1)

    def tile(h):
        return pl.ds(pl.multiple_of(lax.rem(h, half) * 128, 128), 128)

    def line(h):
        return pl.ds(lax.rem(h, half), 1)

    kext[WIN : WIN + tok] = k_ref[...]
    vext[WIN : WIN + tok] = v_ref[...]
    vt = v_ref[...].astype(F32).T.astype(BF16)
    vt2 = lanes(vt, vt)

    def own_keys(scan):
        def own_keys(h, carry):
            phi = maps(k_ref[...], wk_ref[h])
            hi, lo = split(phi)
            pkh[h, WIN : WIN + tok] = hi
            pkl[h, WIN : WIN + tok] = lo
            scan.own[tile(h)] = nn(vt2, rows(hi, lo))
            scan.own_norm[line(h)] = jnp.sum(phi, axis=0, keepdims=True)
            return carry

        return own_keys

    fwd_a.own_norm[...] = jnp.zeros((16, 128), F32)
    fwd_b.own_norm[...] = jnp.zeros((16, 128), F32)
    bwd_a.own_norm[...] = jnp.zeros((16, 128), F32)
    bwd_b.own_norm[...] = jnp.zeros((16, 128), F32)
    each(0, half, own_keys(fwd_a))
    each(half, heads, own_keys(fwd_b))

    load_q.wait()
    tmp[...] = q_ref[...].astype(F32)

    def query_maps(h, carry):
        f = tmp[pl.ds(h, tok, stride=heads), :]
        x = f.astype(BF16)
        qh[h] = x
        qt[h] = f.T.astype(BF16)
        hi, lo = split(maps(x, wq_ref[h]))
        pqh[h] = hi
        pql[h] = lo
        return carry

    each(0, heads, query_maps)
    pl.semaphore_wait(barrier, n - 1 + m - 1)

    def edge_copy(i, dev):
        src, dst = (k_ref, kext) if i == 0 else (v_ref, vext)
        return remote(src.at[pl.ds(tok - WIN, WIN)], dst.at[pl.ds(0, WIN)], e_sems.at[0, i], e_sems.at[1, i], dev)

    @pl.when(me < n - 1)
    def _():
        edge_copy(0, me + 1).start()
        edge_copy(1, me + 1).start()


    fwd_a.start()
    fwd_b.start()

    @pl.when(me == 0)
    def _():
        kext[0:WIN] = jnp.zeros((WIN, 128), BF16)
        vext[0:WIN] = jnp.zeros((WIN, 128), BF16)

    @pl.when(me > 0)
    def _():
        edge_copy(0, me - 1).wait_recv()
        edge_copy(1, me - 1).wait_recv()

    pad = jnp.zeros((WIN, 128), BF16)
    kext[WIN + tok :] = pad
    vext[WIN + tok :] = pad
    valid = jnp.where(me > 0, 1.0, 0.0).astype(F32)
    vaug[:, 0:128] = vext[...]
    vaug[:, 128:256] = jnp.ones((tok + 2 * WIN, 128), BF16)
    vaugt[0:128] = vext[0:tok].astype(F32).T.astype(BF16)
    vaugt[128:256] = jnp.ones((128, tok), BF16)
    kt[...] = kext[0:tok].astype(F32).T.astype(BF16)

    def edge_maps(h, carry):
        phi = maps(kext[0:WIN], wk_ref[h]) * valid
        hi, lo = split(phi)
        pkh[h, 0:WIN] = hi
        pkl[h, 0:WIN] = lo
        return carry

    each(0, heads, edge_maps)

    r2 = lax.broadcasted_iota(jnp.int32, (BLK, 2 * BLK), 0)
    c2 = lax.broadcasted_iota(jnp.int32, (BLK, 2 * BLK), 1)
    near_band = (c2 > r2) & (c2 <= r2 + WIN)
    first_key = jnp.where(me > 0, 0, WIN)
    r1 = lax.broadcasted_iota(jnp.int32, (BLK, BLK), 0)
    c1 = lax.broadcasted_iota(jnp.int32, (BLK, BLK), 1)
    causal = c1 <= r1

    def local_forward(h, carry):
        ph0 = pkh[h, 0:WIN]
        pl0 = pkl[h, 0:WIN]
        zero = jnp.zeros((WIN, 128), BF16)
        vb = vaugt[:, 0:BLK]
        state = -nn(lanes(vb, vb), rows(ph0, zero, pl0, zero))
        for b in range(nblk):
            at = b * BLK
            loc[h, b] = state[0:128]
            loc_norm[h, b] = state[128:136]
            kh = pkh[h, at : at + BLK]
            kl = pkl[h, at : at + BLK]
            qhi = pqh[h, at : at + BLK]
            qlo = pql[h, at : at + BLK]
            q3 = lanes(qhi, qlo, qhi)
            far = jnp.where(causal, nt(q3, lanes(kh, kh, kl)), 0.0)
            s = nt(qh[h, at : at + BLK], kext[at : at + 2 * BLK]) * scale
            mask = near_band & (c2 >= first_key) if b == 0 else near_band
            s = jnp.where(mask, s, -1e30)
            top = jnp.max(s, axis=-1, keepdims=True)
            w = jnp.where(mask, jnp.exp(s - top), 0.0)
            w = lanes(w[:, 0:BLK] + far, w[:, BLK:])
            whi, wlo = split(w)
            va = vaug[at : at + 2 * BLK]
            shi, slo = split(state)
            numer[h, at : at + BLK] = nn(lanes(whi, wlo), rows(va, va)) + nt(q3, lanes(shi, shi, slo))
            if b + 1 < nblk:
                vb = vaugt[:, at : at + BLK]
                state = state + nn(lanes(vb, vb), rows(kh, kl))
        return carry

    each(0, half, local_forward, unroll=4)
    fwd_a.turn()
    each(half, half + 2, local_forward)
    fwd_b.turn()
    each(half + 2, heads, local_forward)

    load_t.wait()
    tmp[...] = t_ref[...].astype(F32)

    def outputs(h, squares, fwd, bwd):
        prior = fwd.out[tile(h)]
        prior_norm = jnp.broadcast_to(fwd.out_norm[line(h)], (128, 128))
        shi, slo = split(rows(prior, prior_norm))
        s3 = lanes(shi, shi, slo)
        d_sum = jnp.zeros((128, 128), F32)
        dn_sum = jnp.zeros((1, 128), F32)
        for b in range(nblk):
            at = b * BLK
            qhi = pqh[h, at : at + BLK]
            qlo = pql[h, at : at + BLK]
            both = numer[h, at : at + BLK] + nt(lanes(qhi, qlo, qhi), s3)
            den = both[:, 128:256]
            y = both[:, 0:128] / den
            where = pl.ds(h + at * heads, BLK, stride=heads)
            error = y - tmp[where, :]
            tmp[where, :] = y
            squares = squares + jnp.sum((error * error).reshape(BLK // 8, 8, 128), axis=0)
            gn = (2.0 * inv_total) * error / den
            gd = jnp.broadcast_to(-jnp.sum(gn * y, axis=-1, keepdims=True), (BLK, 128))
            gn_s[h, at : at + BLK] = gn
            gd_s[h, at : at + BLK] = gd
            ghi, glo = split(gn.T)
            d = nn(lanes(ghi, glo, ghi), rows(qhi, qhi, qlo))
            dn = jnp.sum(gd * (qhi.astype(F32) + qlo.astype(F32)), axis=0, keepdims=True)
            dblk[h, b] = d
            dblk_norm[h, b] = jnp.broadcast_to(dn, (8, 128))
            d_sum = d_sum + d
            dn_sum = dn_sum + dn
        bwd.own[tile(h)] = d_sum
        bwd.own_norm[line(h)] = dn_sum
        return squares

    def half_outputs(lo, fwd, bwd):
        fwd.finish()
        bwd.own_norm[8:16] = each(lo, lo + half, lambda h, c: outputs(h, c, fwd, bwd), jnp.zeros((8, 128), F32), 4)
        bwd.start()

    half_outputs(0, fwd_a, bwd_a)
    half_outputs(half, fwd_b, bwd_b)

    def loss_cols(dev, src):
        return remote(loss_row, loss_kv.at[src], lk_sems.at[0, dev], lk_sems.at[1, src], dev, "kvh")

    y_ref[...] = tmp[...].astype(BF16)
    save_y.start()

    def local_backward(h, carry, fwd):
        prior = fwd.out[tile(h)]
        prior_norm = fwd.out_norm[line(h)]
        later = jnp.zeros((128, 128), F32)
        later_norm = jnp.zeros((1, 128), F32)
        g = jnp.zeros((128, 128), F32)
        for b in reversed(range(nblk)):
            at = b * BLK
            gn = gn_s[h, at : at + BLK]
            gd = gd_s[h, at : at + BLK]
            vb = vext[at : at + BLK]
            kh = pkh[h, at : at + BLK]
            kl = pkl[h, at : at + BLK]
            qhi = pqh[h, at : at + BLK]
            qlo = pql[h, at : at + BLK]
            ghi, glo = split(gn)
            gf = jnp.where(causal, nt(lanes(ghi, glo), lanes(vb, vb)) + gd, 0.0)
            fhi, flo = split(gf)
            shi, slo = split(prior + loc[h, b])
            norm = prior_norm + loc_norm[h, b, 0:1]
            gqf = nn(lanes(fhi, flo, fhi, ghi, glo, ghi), rows(kh, kh, kl, shi, shi, slo)) + gd * norm
            rhi, rlo = split(back(qhi.astype(F32) + qlo.astype(F32), gqf))
            qtb = qt[h, :, at : at + BLK]
            g = g + nn(lanes(qtb, qtb), rows(rhi, rlo))
            thi, tlo = split(gf.T)
            lhi, llo = split(later)
            gkf[h, at : at + BLK] = (
                nn(lanes(thi, tlo, thi, vb, vb), rows(qhi, qhi, qlo, lhi, llo)) + later_norm
            )
            later = later + dblk[h, b]
            later_norm = later_norm + dblk_norm[h, b, 0:1]
        put(aq, h, g)
        return carry

    def put(ref, h, g):
        g = g.T
        ref[pl.ds(pl.multiple_of(h * 64, 64), 64)] = g[0:64] - g[64:128]

    def backward_a(h, carry):
        return local_backward(h, carry, fwd_a)

    def backward_b(h, carry):
        return local_backward(h, carry, fwd_b)

    each(0, 2, backward_a)
    bwd_a.turn()
    each(2, half, backward_a)
    bwd_b.turn()
    each(half, heads, backward_b, unroll=4)
    q_total = Total(n, me, aq, aq_got, aq_part, aq_out, q_sems)
    k_total = Total(n, me, ak, ak_got, ak_part, ak_out, k_sems)
    q_total.start()

    def key_grads(h, carry, bwd):
        shi, slo = split(bwd.out[tile(h)])
        v = vext[0:tok]
        g = gkf[h] + nn(lanes(v, v), rows(shi, slo)) + bwd.out_norm[line(h)]
        hi, lo = split(back(pkh[h, 0:tok].astype(F32) + pkl[h, 0:tok].astype(F32), g))
        t = kt[...]
        put(ak, h, nn(lanes(t, t), rows(hi, lo)))
        return carry

    bwd_a.finish()
    each(0, half, lambda h, c: key_grads(h, c, bwd_a))
    bwd_b.finish()
    loss_row[...] = bwd_a.out_norm[8:16] + bwd_b.out_norm[8:16]
    peers(m, lambda i: loss_cols(lax.rem(col + i, m), col).start())
    each(half, heads, lambda h, c: key_grads(h, c, bwd_b))
    k_total.start()
    q_total.turn()
    k_total.turn()

    loss_kv[col] = loss_row[...]
    peers(m, lambda i: loss_cols(col, lax.rem(col + i, m)).wait_recv())
    total = lax.fori_loop(0, m, lambda i, t: t + loss_kv[i], jnp.zeros((8, 128), F32))
    loss_ref[0, 0] = jnp.sum(total) * inv_total

    q_total.finish()
    gq_ref[...] = aq_out[...]

    fwd_a.drain()
    fwd_b.drain()
    bwd_a.drain()
    bwd_b.drain()

    @pl.when(me < n - 1)
    def _():
        edge_copy(0, me + 1).wait_send()
        edge_copy(1, me + 1).wait_send()

    peers(m, lambda i: loss_cols(lax.rem(col + i, m), col).wait_send())
    save_y.wait()
    k_total.finish()
    gk_ref[...] = ak_out[...]
    q_total.drain()
    k_total.drain()


def body(queries, keys, values, teacher, q_map, k_map):
    tok, heads, width = queries.shape
    n, m = lax.axis_size("seq"), lax.axis_size("kvh")
    nblk = tok // BLK
    vmem = lambda shape, dtype=F32: pltpu.VMEM(shape, dtype)
    dma = lambda *shape: pltpu.SemaphoreType.DMA(shape)
    state = heads // 2 * 128
    grad = heads * 64
    scan_bufs = lambda: [
        vmem((state, 128)),
        vmem((16, 128)),
        vmem((n, state // n, 128)),
        vmem((n, state // n, 128)),
        vmem((state, 128)),
        vmem((n, 16, 128)),
        vmem((n, 16, 128)),
        vmem((16, 128)),
    ]
    total_bufs = lambda: [vmem((grad, 128)), vmem((n, grad // n, 128)), vmem((grad // n, 128)), vmem((grad, 128))]
    spec = pl.BlockSpec(memory_space=pltpu.VMEM)
    hbm = pl.BlockSpec(memory_space=pl.ANY)
    outs, grad_q, grad_k, loss = pl.pallas_call(
        functools.partial(kernel, n, m, heads, tok, width**-0.5, 1.0 / (tok * n)),
        out_shape=(
            jax.ShapeDtypeStruct((tok * heads, width), BF16),
            jax.ShapeDtypeStruct((grad, width), F32),
            jax.ShapeDtypeStruct((grad, width), F32),
            jax.ShapeDtypeStruct((1, 1), F32),
        ),
        in_specs=[hbm, spec, spec, hbm, spec, spec],
        out_specs=(hbm, spec, spec, pl.BlockSpec(memory_space=pltpu.SMEM)),
        scratch_shapes=[
            vmem((tok * heads, width)),
            vmem((tok + 2 * WIN, 128), BF16),
            vmem((tok + 2 * WIN, 128), BF16),
            vmem((tok + 2 * WIN, 256), BF16),
            vmem((256, tok), BF16),
            vmem((128, tok), BF16),
            vmem((heads, tok, 128), BF16),
            vmem((heads, 128, tok), BF16),
            vmem((heads, tok, 128), BF16),
            vmem((heads, tok, 128), BF16),
            vmem((heads, tok + WIN, 128), BF16),
            vmem((heads, tok + WIN, 128), BF16),
            scan_bufs(),
            scan_bufs(),
            vmem((heads, nblk, 128, 128)),
            vmem((heads, nblk, 8, 128)),
            vmem((heads, tok, 256)),
            vmem((heads, tok, 128)),
            vmem((heads, tok, 128)),
            vmem((heads, nblk, 128, 128)),
            vmem((heads, nblk, 8, 128)),
            scan_bufs(),
            scan_bufs(),
            vmem((heads, tok, 128)),
            *total_bufs(),
            *total_bufs(),
            vmem((8, 128)),
            vmem((m, 8, 128)),
            vmem((tok * heads, width), BF16),
            vmem((tok * heads, width), BF16),
            vmem((tok * heads, width), BF16),
            (dma(4), dma(4)),
            (dma(4), dma(4)),
            (dma(4), dma(4)),
            (dma(4), dma(4)),
            dma(4),
            dma(4),
            dma(2, 2),
            dma(2, m),
            dma(3),
        ],
        compiler_params=pltpu.CompilerParams(collective_id=1, has_side_effects=True, vmem_limit_bytes=58 << 20),
    )(
        queries.reshape(tok * heads, width),
        keys.reshape(tok, width),
        values.reshape(tok, width),
        teacher.reshape(tok * heads, width),
        jnp.swapaxes(q_map, 1, 2),
        jnp.swapaxes(k_map, 1, 2),
    )
    unmap = lambda g: jnp.swapaxes(g.reshape(heads, 64, width), 1, 2)
    return outs.reshape(tok, heads, width), unmap(grad_q), unmap(grad_k), loss.reshape(())


def solution(mesh):
    in_specs = (
        P("seq", "kvh", None),
        P("seq", "kvh", None),
        P("seq", "kvh", None),
        P("seq", "kvh", None),
        P("kvh", None, None),
        P("kvh", None, None),
    )
    out_specs = (P("seq", "kvh", None), P("kvh", None, None), P("kvh", None, None), P())
    return jax.shard_map(body, mesh=mesh, in_specs=in_specs, out_specs=out_specs, check_vma=False)
```
